512 devices in a mesh: gx: 16 (over z, core), gy: 32 (over x, y).
Axes of the slice: x: 4, y: 8, z: 8, core: 2. Of those that a mesh axis runs over, the one named last changes fastest.
Arguments:
- points_in: bfloat16 [16, 1048576], P(None, ('gx', 'gy')), may hold values from -6 to 6
- near_blocks: bfloat16 [16384, 64, 256], P(('gx', 'gy')), may hold values from -0.375 to 0.375
- near_source: int32 [16384, 4], P(('gx', 'gy')), may hold values from 0 to 16383, as said below
- near_count: int32 [16384], P(('gx', 'gy')), may hold values from 1 to 4
- col_basis: bfloat16 [64, 1048576], P(None, ('gx', 'gy')), may hold values from -0.75 to 0.75
- row_basis: bfloat16 [64, 1048576], P(None, ('gx', 'gy')), may hold values from -0.75 to 0.75
- up_transfer: bfloat16 [16384, 64, 64], P(('gx', 'gy')), may hold values from -0.125 to 0.125
- down_transfer: bfloat16 [16384, 64, 64], P(('gx', 'gy')), may hold values from -0.75 to 0.75
- leaf_rank: int32 [16384], P(('gx', 'gy')), may hold values from 32 to 64
- kind_table: bfloat16 [16, 64, 64], replicated, may hold values from -0.375 to 0.375
- far_source: int32 [16384, 4], P(('gx', 'gy')), may hold values from 0 to 16383, as said below
- far_kind: int32 [16384, 4], P(('gx', 'gy')), may hold values from 0 to 15
- root_rank: int32 [512], P(('gx', 'gy')), may hold values from 32 to 64
- root_coupling: bfloat16 [512, 8, 64, 64], P(('gx', 'gy')), may hold values from -0.25 to 0.25
- root_source: int32 [512, 8], P(('gx', 'gy')), may hold values from 0 to 31, as said below
- plane_up: bfloat16 [512, 64, 64], P(('gx', 'gy')), may hold values from -0.75 to 0.75
- plane_down: bfloat16 [512, 64, 64], P(('gx', 'gy')), may hold values from -0.75 to 0.75
- plane_coupling: bfloat16 [16, 16, 64, 64], P('gx'), may hold values from -0.03125 to 0.03125
Outputs:
- product: bfloat16 [16, 1048576], P(None, ('gx', 'gy'))
The draws below stay inside these ranges and needn't reach their ends.
Inputs may be any that keep to these rules, and one draw needn't show every extreme that they name: `near_source`: slot 0 of each leaf is the leaf itself; every other slot names a leaf of the same root, or one of the last 16 leaves of the root with the next lower gy index, or one of the first 16 leaves of the root with the next higher gy index (same gx index). `far_source`: each source is a leaf of the root with the same gy index and a gx index one lower or one higher. `root_source`: A root's sources differ from its own gy index, and from the two next to it, modulo 32.
All inputs are finite; a program needn't handle non-finite values.
Results may differ from the reference program's by a relative error of at most 0.007.
Values may be sent and summed in bfloat16 or wider, within the bound.
A program may use at most 64 MiB of HBM per device.

```python
import jax
import jax.numpy as jnp
from jax import lax

LEAF = 64
RANK = 64
RHS = 16
LEAF_DEV = 32
NEAR_SLOTS = 4
FAR_SLOTS = 4
KINDS = 16
ROOT_SLOTS = 8
BORDER = 16
PLANES = 16
PLANE_ROOTS = 32
ROOTS = 512
LEAVES = 16384
POINTS = 1048576


def draw_near_source(key, part):
    key = jax.random.fold_in(key, 11)
    first_key, second_key, third_key = jax.random.split(key, 3)
    leaves = jnp.arange(LEAVES, dtype=jnp.int32)[:, None]
    device = leaves // LEAF_DEV
    row_place = device % PLANE_ROOTS
    sides = jax.random.randint(first_key, (LEAVES, NEAR_SLOTS), 0, 3)
    inside = device * LEAF_DEV + jax.random.randint(second_key, (LEAVES, NEAR_SLOTS), 0, LEAF_DEV)
    offset = jax.random.randint(third_key, (LEAVES, NEAR_SLOTS), 0, BORDER)
    lower = (device - 1) * LEAF_DEV + LEAF_DEV - BORDER + offset
    upper = (device + 1) * LEAF_DEV + offset
    picked = jnp.where((sides == 1) & (row_place > 0), lower, jnp.where((sides == 2) & (row_place < PLANE_ROOTS - 1), upper, inside))
    slots = jnp.arange(NEAR_SLOTS, dtype=jnp.int32)[None, :]
    return jnp.where(slots == 0, leaves, picked).astype(jnp.int32)


def draw_far_source(key, part):
    key = jax.random.fold_in(key, 23)
    first_key, second_key = jax.random.split(key, 2)
    leaves = jnp.arange(LEAVES, dtype=jnp.int32)[:, None]
    device = leaves // LEAF_DEV
    plane = device // PLANE_ROOTS
    stride = jnp.where(jax.random.randint(first_key, (LEAVES, FAR_SLOTS), 0, 2) == 0, -1, 1)
    stride = jnp.where(plane == 0, 1, jnp.where(plane == PLANES - 1, -1, stride))
    source_device = device + stride * PLANE_ROOTS
    return (source_device * LEAF_DEV + jax.random.randint(second_key, (LEAVES, FAR_SLOTS), 0, LEAF_DEV)).astype(jnp.int32)


def draw_root_source(key, part):
    key = jax.random.fold_in(key, 37)
    roots = jnp.arange(ROOTS, dtype=jnp.int32)[:, None]
    row_place = roots % PLANE_ROOTS
    step_size = jax.random.randint(key, (ROOTS, ROOT_SLOTS), 0, PLANE_ROOTS - 3)
    return ((row_place + 2 + step_size) % PLANE_ROOTS).astype(jnp.int32)


def place_ends(array, rng, smallest, top_value):
    longest = array.shape.index(max(array.shape))
    spots = []
    for shift in (0, 1):
        where = [jax.random.randint(jax.random.fold_in(rng, axis), (), 0, length) for axis, length in enumerate(array.shape)]
        where[longest] = (where[longest] + shift) % array.shape[longest]
        spots.append(tuple(where))
    return array.at[spots[0]].set(smallest).at[spots[1]].set(top_value)


def block_levels(stream_key, shape, pieces, smallest, high):
    factor_of = 1.0
    for dim, shards_of in pieces:
        steps = jax.random.uniform(jax.random.fold_in(jax.random.fold_in(stream_key, 6), dim), (shards_of,), jnp.float32, smallest / len(pieces), high / len(pieces))
        factor_of = factor_of * jnp.repeat(jnp.exp(steps), shape[dim] // shards_of).reshape((-1,) + (1,) * (len(shape) - 1 - dim))
    return factor_of


def scatter_about(own_key, dims, spread, reach, shards=(), held_as=jnp.bfloat16):
    array = spread * jax.random.normal(own_key, dims, jnp.float32)
    if shards:
        array = array * block_levels(own_key, dims, shards, -0.22, 0.18)
    return jnp.clip(array, -reach, reach).astype(held_as)


def setup_inputs(seed: int = 0) -> dict:
    key_list = jax.random.split(jax.random.key(seed), 19)
    return {
        "points_in": scatter_about(key_list[0], (RHS, POINTS), 1.0, 6.0, ((1, 512),)),
        "near_blocks": scatter_about(key_list[1], (LEAVES, LEAF, NEAR_SLOTS * LEAF), (NEAR_SLOTS * LEAF) ** -0.5, 0.375, ((0, 512),)),
        "near_source": draw_near_source(jax.random.fold_in(key_list[18], 71), 0),
        "near_count": place_ends(jax.random.randint(key_list[3], (LEAVES,), 1, NEAR_SLOTS + 1), jax.random.fold_in(key_list[3], 1), 1, NEAR_SLOTS).astype(jnp.int32),
        "col_basis": scatter_about(key_list[4], (RANK, POINTS), LEAF ** -0.5, 0.75, ((1, 512),)),
        "row_basis": scatter_about(key_list[5], (RANK, POINTS), RANK ** -0.5, 0.75, ((1, 512),)),
        "up_transfer": scatter_about(key_list[6], (LEAVES, RANK, RANK), (RANK * LEAF_DEV) ** -0.5, 0.125, ((0, 512),)),
        "down_transfer": scatter_about(key_list[7], (LEAVES, RANK, RANK), RANK ** -0.5, 0.75, ((0, 512),)),
        "leaf_rank": place_ends(jax.random.randint(key_list[8], (LEAVES,), RANK // 2, RANK + 1), jax.random.fold_in(key_list[8], 1), RANK // 2, RANK).astype(jnp.int32),
        "kind_table": scatter_about(key_list[9], (KINDS, RANK, RANK), (RANK * FAR_SLOTS) ** -0.5, 0.375),
        "far_source": draw_far_source(jax.random.fold_in(key_list[18], 71), 0),
        "far_kind": place_ends(jax.random.randint(key_list[11], (LEAVES, FAR_SLOTS), 0, KINDS), jax.random.fold_in(key_list[11], 1), 0, KINDS - 1).astype(jnp.int32),
        "root_rank": place_ends(jax.random.randint(key_list[12], (ROOTS,), RANK // 2, RANK + 1), jax.random.fold_in(key_list[12], 1), RANK // 2, RANK).astype(jnp.int32),
        "root_coupling": scatter_about(key_list[13], (ROOTS, ROOT_SLOTS, RANK, RANK), (RANK * ROOT_SLOTS) ** -0.5, 0.25, ((0, 512),)),
        "root_source": draw_root_source(jax.random.fold_in(key_list[18], 71), 0),
        "plane_up": scatter_about(key_list[15], (ROOTS, RANK, RANK), RANK ** -0.5, 0.75, ((0, 512),)),
        "plane_down": scatter_about(key_list[16], (ROOTS, RANK, RANK), RANK ** -0.5, 0.75, ((0, 512),)),
        "plane_coupling": scatter_about(key_list[17], (PLANES, PLANES, RANK, RANK), (RANK * PLANES * PLANE_ROOTS) ** -0.5, 0.03125, ((0, 16),)),
    }


highest = lax.Precision.HIGHEST


def rank_keep(ranks):
    return jnp.arange(RANK, dtype=jnp.int32)[None, :] < ranks[:, None]


def reference(points_in, near_blocks, near_source, near_count, col_basis, row_basis, up_transfer, down_transfer, leaf_rank, kind_table, far_source, far_kind, root_rank, root_coupling, root_source, plane_up, plane_down, plane_coupling):
    span = LEAF_DEV * LEAF
    points_three = points_in.reshape(RHS, LEAVES, LEAF)

    def upward(device):
        start = (device * span).astype(jnp.int32)
        first = (device * LEAF_DEV).astype(jnp.int32)
        local = lax.dynamic_slice_in_dim(points_in, start, span, 1).reshape(RHS, LEAF_DEV, LEAF).astype(jnp.float32)
        basis = lax.dynamic_slice_in_dim(col_basis, start, span, 1).reshape(RANK, LEAF_DEV, LEAF).astype(jnp.float32)
        coeffs = jnp.einsum("klp,rlp->lkr", basis, local, precision=highest)
        ranks = lax.dynamic_slice_in_dim(leaf_rank, first, LEAF_DEV, 0)
        coeffs = jnp.where(rank_keep(ranks)[:, :, None], coeffs, jnp.float32(0.0)).astype(jnp.bfloat16)
        transfer = lax.dynamic_slice_in_dim(up_transfer, first, LEAF_DEV, 0).astype(jnp.float32)
        root = jnp.einsum("lkj,lkr->jr", transfer, coeffs.astype(jnp.float32), precision=highest)
        return coeffs, root

    coeffs_all, roots_raw = lax.map(upward, jnp.arange(ROOTS, dtype=jnp.int32))
    root_keep = rank_keep(root_rank)
    roots = jnp.where(root_keep[:, :, None], roots_raw, jnp.float32(0.0)).astype(jnp.bfloat16)
    partial_value = jnp.einsum("dji,djr->dir", plane_up.astype(jnp.float32), roots.astype(jnp.float32), precision=highest)
    plane_values = partial_value.reshape(PLANES, PLANE_ROOTS, RANK, RHS).sum(axis=1)
    plane_ids = jnp.arange(PLANES, dtype=jnp.int32)
    far_mask = (jnp.abs(plane_ids[:, None] - plane_ids[None, :]) >= 2).astype(jnp.float32)
    plane_out = jnp.einsum("pqij,pq,qjr->pir", plane_coupling.astype(jnp.float32), far_mask, plane_values, precision=highest)
    devices = jnp.arange(ROOTS, dtype=jnp.int32)
    source_root = (devices // PLANE_ROOTS)[:, None] * PLANE_ROOTS + root_source
    chosen = roots[source_root].astype(jnp.float32)
    root_out = jnp.einsum("dcjk,dckr->djr", root_coupling.astype(jnp.float32), chosen, precision=highest)
    root_out = root_out + jnp.einsum("dji,dir->djr", plane_down.astype(jnp.float32), plane_out[devices // PLANE_ROOTS], precision=highest)
    root_out = jnp.where(root_keep[:, :, None], root_out, jnp.float32(0.0)).astype(jnp.bfloat16)
    coeffs_flat = coeffs_all.reshape(LEAVES, RANK, RHS)

    def downward(device):
        start = (device * span).astype(jnp.int32)
        first = (device * LEAF_DEV).astype(jnp.int32)
        far_rows = lax.dynamic_slice_in_dim(far_source, first, LEAF_DEV, 0)
        kind_rows = lax.dynamic_slice_in_dim(far_kind, first, LEAF_DEV, 0)
        sources = jnp.take(coeffs_flat, far_rows.reshape(-1), axis=0).reshape(LEAF_DEV, FAR_SLOTS, RANK, RHS).astype(jnp.float32)
        matrices = jnp.take(kind_table, kind_rows.reshape(-1), axis=0).reshape(LEAF_DEV, FAR_SLOTS, RANK, RANK).astype(jnp.float32)
        leaf_out = jnp.einsum("lcjk,lckr->ljr", matrices, sources, precision=highest)
        transfer = lax.dynamic_slice_in_dim(down_transfer, first, LEAF_DEV, 0).astype(jnp.float32)
        leaf_out = leaf_out + jnp.einsum("lkj,jr->lkr", transfer, root_out[device].astype(jnp.float32), precision=highest)
        ranks = lax.dynamic_slice_in_dim(leaf_rank, first, LEAF_DEV, 0)
        leaf_out = jnp.where(rank_keep(ranks)[:, :, None], leaf_out, jnp.float32(0.0)).astype(jnp.bfloat16)
        basis = lax.dynamic_slice_in_dim(row_basis, start, span, 1).reshape(RANK, LEAF_DEV, LEAF).astype(jnp.float32)
        far_part = jnp.einsum("klp,lkr->rlp", basis, leaf_out.astype(jnp.float32), precision=highest)
        near_rows = lax.dynamic_slice_in_dim(near_source, first, LEAF_DEV, 0)
        counts = lax.dynamic_slice_in_dim(near_count, first, LEAF_DEV, 0)
        gathered = jnp.take(points_three, near_rows.reshape(-1), axis=1).reshape(RHS, LEAF_DEV, NEAR_SLOTS, LEAF)
        live_slots = jnp.arange(NEAR_SLOTS, dtype=jnp.int32)[None, :] < counts[:, None]
        gathered = jnp.where(live_slots[None, :, :, None], gathered.astype(jnp.float32), jnp.float32(0.0))
        blocks = lax.dynamic_slice_in_dim(near_blocks, first, LEAF_DEV, 0).reshape(LEAF_DEV, LEAF, NEAR_SLOTS, LEAF).astype(jnp.float32)
        near_part = jnp.einsum("rlnq,lpnq->rlp", gathered, blocks, precision=highest)
        return (near_part + far_part).astype(jnp.bfloat16).reshape(RHS, span)

    result = lax.map(downward, devices)
    return jnp.transpose(result, (1, 0, 2)).reshape(RHS, POINTS)
```

```python
import jax
import jax.numpy as jnp
from jax import lax
from jax.experimental import pallas as pl
from jax.experimental.pallas import tpu as pltpu
from jax.sharding import PartitionSpec as P

MESH = pl.DeviceIdType.MESH
BF = jnp.bfloat16
F32 = jnp.float32

RHS = 16
LEAVES = 32
RANK = 64
BORDER = 16
GX = 16
GY = 32
NEAR = 4
FAR = 4
KINDS = 16
ROOT_SLOTS = 8
CHUNKS = 8
SPAN = LEAVES * RANK


def dot_nt(a, b):
    return lax.dot_general(a, b, (((1,), (1,)), ((), ())), preferred_element_type=F32)


def dot_nn(a, b):
    return lax.dot_general(a, b, (((1,), (0,)), ((), ())), preferred_element_type=F32)


def kernel(
    points,
    col,
    up,
    plane_up,
    plane_coupling,
    near_blocks,
    kind_table,
    row,
    root_coupling,
    down,
    plane_down,
    near_source,
    near_count,
    leaf_rank,
    far_source,
    far_kind,
    root_rank,
    root_source,
    out,
    points_v,
    col_v,
    up_v,
    pu_v,
    pc_v,
    near_v,
    kind_v,
    row_v,
    rc_v,
    down_v,
    pd_v,
    points_halo,
    coef,
    coef_halo,
    part_buf,
    root_buf,
    sum_buf,
    near_left,
    near_right,
    far_left,
    far_right,
    kind_left,
    kind_right,
    pc_cat,
    rc_cat,
    row_diag,
    keep_lanes,
    far_rows,
    near_rows,
    load_sem,
    halo_send,
    halo_recv,
    gather_send,
    gather_recv,
):
    gx = lax.axis_index("gx")
    gy = lax.axis_index("gy")
    first_leaf = (gx * GY + gy) * LEAVES

    loads = []
    for place, (src, dst) in enumerate(
        (
            (points, points_v),
            (col, col_v),
            (up, up_v),
            (plane_up.at[0], pu_v),
            (plane_coupling.at[0], pc_v),
            (near_blocks, near_v),
            (kind_table, kind_v),
            (row, row_v),
            (root_coupling.at[0], rc_v),
            (down, down_v),
            (plane_down.at[0], pd_v),
        )
    ):
        loads.append(pltpu.make_async_copy(src, dst, load_sem.at[place]))
        loads[-1].start()
    (
        load_points,
        load_col,
        load_up,
        load_pu,
        load_pc,
        load_near,
        load_kind,
        load_row,
        load_rc,
        load_down,
        load_pd,
    ) = loads

    barrier = pltpu.get_barrier_semaphore()

    def greet_gx(i, carry):
        pl.semaphore_signal(
            barrier, inc=1, device_id=(lax.rem(gx + i, GX), gy), device_id_type=MESH
        )
        return carry

    def greet_gy(i, carry):
        pl.semaphore_signal(
            barrier, inc=1, device_id=(gx, lax.rem(gy + i, GY)), device_id_type=MESH
        )
        return carry

    lax.fori_loop(1, GX, greet_gx, 0)
    lax.fori_loop(1, GY, greet_gy, 0)

    lane = lax.broadcasted_iota(jnp.int32, (RHS, 128), 1)
    low = lane < RANK
    left_mask = low.astype(F32).astype(BF)
    right_mask = (lane >= RANK).astype(F32).astype(BF)
    lane_leaf = lax.broadcasted_iota(jnp.int32, (RANK, 256), 1) // RANK
    leaf_masks = [(lane_leaf == i).astype(F32).astype(BF) for i in range(4)]

    def block_diag(block):
        return jnp.concatenate([block * mask for mask in leaf_masks], axis=0)

    def diagonal(full):
        first = jnp.where(low, full[0:16, 0:128], full[16:32, 0:128])
        second = jnp.where(low, full[32:48, 128:256], full[48:64, 128:256])
        return jnp.concatenate([first, second], axis=1)

    lane_rank = lax.broadcasted_iota(jnp.int32, (8, 128), 1)
    in_low = lane_rank < RANK
    rank_of_lane = jnp.where(in_low, lane_rank, lane_rank - RANK)
    for pair in range(LEAVES // 2):
        ranks = jnp.where(in_low, leaf_rank[2 * pair], leaf_rank[2 * pair + 1])
        keep_lanes[:, 128 * pair : 128 * pair + 128] = (rank_of_lane < ranks).astype(F32)

    load_points.wait()
    load_col.wait()
    for c in range(CHUNKS):
        span = slice(256 * c, 256 * c + 256)
        full = dot_nt(points_v[:, span], block_diag(col_v[:, span]))
        keep = jnp.concatenate([keep_lanes[:, span]] * 2, axis=0)
        coef[:, span] = jnp.where(keep > 0.0, full, 0.0).astype(BF)

    load_up.wait()
    root = jnp.zeros((RHS, RANK), F32)
    for c in range(CHUNKS):
        root = root + dot_nn(
            coef[:, 256 * c : 256 * c + 256], up_v[4 * c : 4 * c + 4].reshape(256, RANK)
        )
    root_keep = lax.broadcasted_iota(jnp.int32, (RHS, RANK), 1) < root_rank[0]
    root = jnp.where(root_keep, root, 0.0)
    load_pu.wait()
    part = dot_nn(root.astype(BF), pu_v[...])
    part_buf[gx] = jnp.concatenate([part, part], axis=1).astype(BF)
    root_buf[gy] = jnp.concatenate([root, root], axis=1).astype(BF)

    pl.semaphore_wait(barrier, GX - 1 + GY - 1)

    def spread_gx(buf, place):
        def send(i, carry):
            pltpu.make_async_remote_copy(
                src_ref=buf.at[gx],
                dst_ref=buf.at[gx],
                send_sem=gather_send.at[place],
                recv_sem=gather_recv.at[place],
                device_id=(lax.rem(gx + i, GX), gy),
                device_id_type=MESH,
            ).start()
            return carry

        lax.fori_loop(1, GX, send, 0)

    def spread_gy(buf, place):
        def send(i, carry):
            pltpu.make_async_remote_copy(
                src_ref=buf.at[gy],
                dst_ref=buf.at[gy],
                send_sem=gather_send.at[place],
                recv_sem=gather_recv.at[place],
                device_id=(gx, lax.rem(gy + i, GY)),
                device_id_type=MESH,
            ).start()
            return carry

        lax.fori_loop(1, GY, send, 0)

    def wait_all(sem, buf, count):
        held = buf.at[pl.ds(0, count)]
        pltpu.make_async_copy(held, held, sem).wait()

    spread_gx(part_buf, 0)
    next_gx = (lax.rem(gx + 1, GX), gy)
    last_gx = (lax.rem(gx + GX - 1, GX), gy)
    next_gy = (gx, lax.rem(gy + 1, GY))
    last_gy = (gx, lax.rem(gy + GY - 1, GY))
    half = BORDER * RANK
    halos = []
    for place, (src, dst, device) in enumerate(
        (
            (points_v.at[:, pl.ds(half, half)], points_halo.at[0], next_gy),
            (points_v.at[:, pl.ds(0, half)], points_halo.at[1], last_gy),
            (coef, coef_halo.at[0], next_gx),
            (coef, coef_halo.at[1], last_gx),
        )
    ):
        halos.append(
            pltpu.make_async_remote_copy(
                src_ref=src,
                dst_ref=dst,
                send_sem=halo_send.at[place],
                recv_sem=halo_recv.at[place],
                device_id=device,
                device_id_type=MESH,
            )
        )
        halos[-1].start()
    spread_gy(root_buf, 1)

    load_pc.wait()
    for pair in range(GX // 2):
        blocks = []
        for q in (2 * pair, 2 * pair + 1):
            far = (jnp.abs(gx - q) >= 2).astype(F32).astype(BF)
            blocks.append(pc_v[q] * far)
        pc_cat[:, 128 * pair : 128 * pair + 128] = jnp.concatenate(blocks, axis=1)
    load_kind.wait()
    zero_block = jnp.zeros((RANK, RANK), BF)
    for t in range(KINDS):
        kind_left[t] = jnp.concatenate([kind_v[t], zero_block], axis=1)
        kind_right[t] = jnp.concatenate([zero_block, kind_v[t]], axis=1)
    load_rc.wait()
    for pair in range(ROOT_SLOTS // 2):
        rc_cat[:, 128 * pair : 128 * pair + 128] = jnp.concatenate(
            [rc_v[2 * pair], rc_v[2 * pair + 1]], axis=1
        )

    def expand(x, left, right, place):
        turned = jnp.concatenate([x[:, RANK:], x[:, :RANK]], axis=1)
        left[place] = x * left_mask
        right[place + 1] = x * right_mask
        left[place + 1] = turned * left_mask
        right[place] = turned * right_mask

    for pair in range(LEAVES // 2):
        expand(points_v[:, 128 * pair : 128 * pair + 128], near_left, near_right, BORDER + 2 * pair)
    window = 2 * LEAVES
    near_left[window] = jnp.zeros((RHS, 128), BF)
    near_right[window] = jnp.zeros((RHS, 128), BF)

    wait_all(gather_recv.at[0], part_buf, GX - 1)
    lhs = [
        part_buf[2 * pair] * left_mask + part_buf[2 * pair + 1] * right_mask
        for pair in range(GX // 2)
    ]
    plane = dot_nt(jnp.concatenate(lhs, axis=1), pc_cat[...])
    high = plane.astype(BF).astype(F32)
    sum_buf[gy] = jnp.concatenate([high, plane - high], axis=1).astype(BF)
    spread_gy(sum_buf, 2)

    halos[0].wait_recv()
    halos[1].wait_recv()
    for side in range(2):
        for pair in range(BORDER // 2):
            expand(
                points_halo[side, :, 128 * pair : 128 * pair + 128],
                near_left,
                near_right,
                side * (BORDER + LEAVES) + 2 * pair,
            )
    load_near.wait()
    for c in range(CHUNKS):
        rows = []
        for leaf in range(4 * c, 4 * c + 4):
            count = near_count[leaf]
            places = []
            for slot in range(NEAR):
                place = near_source[slot, leaf] - first_leaf + BORDER
                place = jnp.minimum(jnp.maximum(place, 0), window - 1)
                places.append(jnp.where(slot < count, place, window))
            rows.append(
                jnp.concatenate(
                    [
                        near_left[places[0]] + near_right[places[1]],
                        near_left[places[2]] + near_right[places[3]],
                    ],
                    axis=1,
                )
            )
        full = dot_nt(jnp.concatenate(rows, axis=0), near_v[4 * c : 4 * c + 4].reshape(256, 256))
        near_rows[:, 256 * c : 256 * c + 256] = diagonal(full)

    load_row.wait()
    for c in range(CHUNKS):
        row_diag[c] = block_diag(row_v[:, 256 * c : 256 * c + 256])

    halos[2].wait_recv()
    halos[3].wait_recv()
    for side in range(2):
        for pair in range(LEAVES // 2):
            expand(
                coef_halo[side, :, 128 * pair : 128 * pair + 128],
                far_left,
                far_right,
                side * LEAVES + 2 * pair,
            )
    for c in range(CHUNKS):
        rows = []
        matrices = []
        for leaf in range(4 * c, 4 * c + 4):
            places = []
            kinds = []
            for slot in range(FAR):
                source = far_source[slot, leaf] - first_leaf
                place = jnp.where(
                    source < 0, source + GY * LEAVES, source - GY * LEAVES + LEAVES
                )
                places.append(jnp.minimum(jnp.maximum(place, 0), window - 1))
                kinds.append(far_kind[slot, leaf])
            rows.append(
                jnp.concatenate(
                    [
                        far_left[places[0]] + far_right[places[1]],
                        far_left[places[2]] + far_right[places[3]],
                    ],
                    axis=1,
                )
            )
            matrices.append(
                jnp.concatenate(
                    [
                        kind_left[kinds[0]] + kind_right[kinds[1]],
                        kind_left[kinds[2]] + kind_right[kinds[3]],
                    ],
                    axis=1,
                )
            )
        full = dot_nt(jnp.concatenate(rows, axis=0), jnp.concatenate(matrices, axis=0))
        far_rows[:, 256 * c : 256 * c + 256] = diagonal(full)

    wait_all(gather_recv.at[1], root_buf, GY - 1)
    chosen = [
        root_buf[root_source[0, 2 * pair]] * left_mask
        + root_buf[root_source[0, 2 * pair + 1]] * right_mask
        for pair in range(ROOT_SLOTS // 2)
    ]
    beside = dot_nt(jnp.concatenate(chosen, axis=1), rc_cat[...])
    load_down.wait()
    load_pd.wait()

    wait_all(gather_recv.at[2], sum_buf, GY - 1)
    total = [sum_buf[q].astype(F32) for q in range(GY)]
    while len(total) > 1:
        total = [a + b for a, b in zip(total[0::2], total[1::2])]
    plane_out = total[0][:, :RANK] + total[0][:, RANK:]
    root_out = beside + dot_nt(plane_out.astype(BF), pd_v[...])
    root_out = jnp.where(root_keep, root_out, 0.0).astype(BF)
    for c in range(CHUNKS):
        span = slice(256 * c, 256 * c + 256)
        leaf_out = far_rows[:, span] + dot_nt(
            root_out, down_v[4 * c : 4 * c + 4].reshape(256, RANK)
        )
        keep = jnp.concatenate([keep_lanes[:, span]] * 2, axis=0)
        leaf_out = jnp.where(keep > 0.0, leaf_out, 0.0).astype(BF)
        out[:, span] = (near_rows[:, span] + dot_nn(leaf_out, row_diag[c])).astype(BF)

    for halo in halos:
        halo.wait_send()
    wait_all(gather_send.at[0], part_buf, GX - 1)
    wait_all(gather_send.at[1], root_buf, GY - 1)
    wait_all(gather_send.at[2], sum_buf, GY - 1)


def per_device(
    points_in,
    near_blocks,
    near_source,
    near_count,
    col_basis,
    row_basis,
    up_transfer,
    down_transfer,
    leaf_rank,
    kind_table,
    far_source,
    far_kind,
    root_rank,
    root_coupling,
    root_source,
    plane_up,
    plane_down,
    plane_coupling,
):
    hbm = pl.BlockSpec(memory_space=pl.ANY)
    smem = pl.BlockSpec(memory_space=pltpu.SMEM)
    return pl.pallas_call(
        kernel,
        out_shape=jax.ShapeDtypeStruct((RHS, SPAN), BF),
        in_specs=[hbm] * 11 + [smem] * 7,
        out_specs=pl.BlockSpec(memory_space=pltpu.VMEM),
        scratch_shapes=[
            pltpu.VMEM((RHS, SPAN), BF),
            pltpu.VMEM((RANK, SPAN), BF),
            pltpu.VMEM((LEAVES, RANK, RANK), BF),
            pltpu.VMEM((RANK, RANK), BF),
            pltpu.VMEM((GX, RANK, RANK), BF),
            pltpu.VMEM((LEAVES, RANK, NEAR * RANK), BF),
            pltpu.VMEM((KINDS, RANK, RANK), BF),
            pltpu.VMEM((RANK, SPAN), BF),
            pltpu.VMEM((ROOT_SLOTS, RANK, RANK), BF),
            pltpu.VMEM((LEAVES, RANK, RANK), BF),
            pltpu.VMEM((RANK, RANK), BF),
            pltpu.VMEM((2, RHS, BORDER * RANK), BF),
            pltpu.VMEM((RHS, SPAN), BF),
            pltpu.VMEM((2, RHS, SPAN), BF),
            pltpu.VMEM((GX, RHS, 128), BF),
            pltpu.VMEM((GY, RHS, 128), BF),
            pltpu.VMEM((GY, RHS, 128), BF),
            pltpu.VMEM((2 * LEAVES + 1, RHS, 128), BF),
            pltpu.VMEM((2 * LEAVES + 1, RHS, 128), BF),
            pltpu.VMEM((2 * LEAVES, RHS, 128), BF),
            pltpu.VMEM((2 * LEAVES, RHS, 128), BF),
            pltpu.VMEM((KINDS, RANK, 128), BF),
            pltpu.VMEM((KINDS, RANK, 128), BF),
            pltpu.VMEM((RANK, GX * RANK), BF),
            pltpu.VMEM((RANK, ROOT_SLOTS * RANK), BF),
            pltpu.VMEM((CHUNKS, 256, 256), BF),
            pltpu.VMEM((8, SPAN), F32),
            pltpu.VMEM((RHS, SPAN), F32),
            pltpu.VMEM((RHS, SPAN), F32),
            pltpu.SemaphoreType.DMA((11,)),
            pltpu.SemaphoreType.DMA((4,)),
            pltpu.SemaphoreType.DMA((4,)),
            pltpu.SemaphoreType.DMA((3,)),
            pltpu.SemaphoreType.DMA((3,)),
        ],
        compiler_params=pltpu.CompilerParams(
            collective_id=0, has_side_effects=True, vmem_limit_bytes=32 * 2**20
        ),
        name="h2_product",
    )(
        points_in,
        col_basis,
        up_transfer,
        plane_up,
        plane_coupling,
        near_blocks,
        kind_table,
        row_basis,
        root_coupling,
        down_transfer,
        plane_down,
        near_source.T,
        near_count,
        leaf_rank,
        far_source.T,
        far_kind.T,
        root_rank,
        root_source,
    )


def solution(mesh):
    return jax.shard_map(
        per_device,
        mesh=mesh,
        in_specs=(
            P(None, ("gx", "gy")),
            P(("gx", "gy"), None, None),
            P(("gx", "gy"), None),
            P(("gx", "gy")),
            P(None, ("gx", "gy")),
            P(None, ("gx", "gy")),
            P(("gx", "gy"), None, None),
            P(("gx", "gy"), None, None),
            P(("gx", "gy")),
            P(),
            P(("gx", "gy"), None),
            P(("gx", "gy"), None),
            P(("gx", "gy")),
            P(("gx", "gy"), None, None, None),
            P(("gx", "gy"), None),
            P(("gx", "gy"), None, None),
            P(("gx", "gy"), None, None),
            P("gx", None, None, None),
        ),
        out_specs=P(None, ("gx", "gy")),
        check_vma=False,
    )
```

```python
import jax
import jax.numpy as jnp
from jax import lax
from jax.experimental import pallas as pl
from jax.experimental.pallas import tpu as pltpu
from jax.sharding import PartitionSpec as P

MESH = pl.DeviceIdType.MESH
BF = jnp.bfloat16
F32 = jnp.float32

RHS = 16
LEAVES = 32
RANK = 64
BORDER = 16
GX = 16
GY = 32
NEAR = 4
FAR = 4
KINDS = 16
ROOT_SLOTS = 8
CHUNKS = 8
SPAN = LEAVES * RANK


def dot_nt(a, b):
    return lax.dot_general(a, b, (((1,), (1,)), ((), ())), preferred_element_type=F32)


def dot_nn(a, b):
    return lax.dot_general(a, b, (((1,), (0,)), ((), ())), preferred_element_type=F32)


def kernel(
    points,
    col,
    up,
    plane_up,
    plane_coupling,
    near_blocks,
    kind_table,
    row,
    root_coupling,
    down,
    plane_down,
    near_source_h,
    near_count_h,
    leaf_rank_h,
    far_source_h,
    far_kind_h,
    root_rank,
    root_source_h,
    out,
    near_source,
    near_count,
    leaf_rank,
    far_source,
    far_kind,
    root_source,
    points_v,
    col_v,
    up_v,
    pu_v,
    pc_v,
    near_v,
    kind_v,
    row_v,
    rc_v,
    down_v,
    pd_v,
    points_halo,
    coef,
    coef_halo,
    part_buf,
    root_buf,
    sum_buf,
    near_left,
    near_right,
    far_left,
    far_right,
    kind_left,
    kind_right,
    pc_cat,
    rc_cat,
    plane_map,
    keep_lanes,
    far_rows,
    near_rows,
    load_sem,
    halo_send,
    halo_recv,
    gather_send,
    gather_recv,
):
    gx = lax.axis_index("gx")
    gy = lax.axis_index("gy")
    first_leaf = (gx * GY + gy) * LEAVES

    pairs = (
        (leaf_rank_h, leaf_rank),
        (points, points_v),
        (col, col_v),
        (up, up_v),
        (plane_up.at[0], pu_v),
        (plane_coupling.at[0], pc_v),
        (near_source_h, near_source),
        (near_count_h, near_count),
        (near_blocks, near_v),
        (kind_table, kind_v),
        (row, row_v),
        (root_coupling.at[0], rc_v),
        (down, down_v),
        (plane_down.at[0], pd_v),
        (far_source_h, far_source),
        (far_kind_h, far_kind),
        (root_source_h, root_source),
    )
    loads = [
        pltpu.make_async_copy(src, dst, load_sem.at[place])
        for place, (src, dst) in enumerate(pairs)
    ]
    (
        load_leaf_rank,
        load_points,
        load_col,
        load_up,
        load_pu,
        load_pc,
        load_near_source,
        load_near_count,
        load_near,
        load_kind,
        load_row,
        load_rc,
        load_down,
        load_pd,
        load_far_source,
        load_far_kind,
        load_root_source,
    ) = loads
    for load in loads[:5]:
        load.start()

    barrier = pltpu.get_barrier_semaphore()

    def greet_gx(i, carry):
        pl.semaphore_signal(
            barrier, inc=1, device_id=(lax.rem(gx + i, GX), gy), device_id_type=MESH
        )
        return carry

    def greet_gy(i, carry):
        pl.semaphore_signal(
            barrier, inc=1, device_id=(gx, lax.rem(gy + i, GY)), device_id_type=MESH
        )
        return carry

    lax.fori_loop(1, GX, greet_gx, 0)
    lax.fori_loop(1, GY, greet_gy, 0)

    lane = lax.broadcasted_iota(jnp.int32, (RHS, 128), 1)
    low = lane < RANK
    left_mask = low.astype(F32).astype(BF)
    right_mask = (lane >= RANK).astype(F32).astype(BF)
    lane_leaf = lax.broadcasted_iota(jnp.int32, (RANK, 256), 1) // RANK
    leaf_masks = [(lane_leaf == i).astype(F32).astype(BF) for i in range(4)]

    def block_diag(block):
        return jnp.concatenate([block * mask for mask in leaf_masks], axis=0)

    def diagonal(full):
        first = jnp.where(low, full[0:16, 0:128], full[16:32, 0:128])
        second = jnp.where(low, full[32:48, 128:256], full[48:64, 128:256])
        return jnp.concatenate([first, second], axis=1)

    lane_rank = lax.broadcasted_iota(jnp.int32, (8, 128), 1)
    in_low = lane_rank < RANK
    rank_of_lane = jnp.where(in_low, lane_rank, lane_rank - RANK)
    load_leaf_rank.wait()
    for pair in range(LEAVES // 2):
        ranks = jnp.where(in_low, leaf_rank[2 * pair], leaf_rank[2 * pair + 1])
        keep_lanes[:, 128 * pair : 128 * pair + 128] = (rank_of_lane < ranks).astype(F32)

    load_points.wait()
    load_col.wait()
    for c in range(CHUNKS):
        span = slice(256 * c, 256 * c + 256)
        full = dot_nt(points_v[:, span], block_diag(col_v[:, span]))
        keep = jnp.concatenate([keep_lanes[:, span]] * 2, axis=0)
        coef[:, span] = jnp.where(keep > 0.0, full, 0.0).astype(BF)

    load_up.wait()
    load_pu.wait()
    for load in loads[5:]:
        load.start()
    root = jnp.zeros((RHS, RANK), F32)
    for c in range(CHUNKS):
        root = root + dot_nn(
            coef[:, 256 * c : 256 * c + 256], up_v[4 * c : 4 * c + 4].reshape(256, RANK)
        )
    root_keep = lax.broadcasted_iota(jnp.int32, (RHS, RANK), 1) < root_rank[0]
    root = jnp.where(root_keep, root, 0.0)
    part = dot_nn(root.astype(BF), pu_v[...])
    part_buf[gx] = jnp.concatenate([part, part], axis=1).astype(BF)
    root_buf[gy] = jnp.concatenate([root, root], axis=1).astype(BF)

    pl.semaphore_wait(barrier, GX - 1 + GY - 1)

    def spread_gx(buf, place):
        def send(i, carry):
            pltpu.make_async_remote_copy(
                src_ref=buf.at[gx],
                dst_ref=buf.at[gx],
                send_sem=gather_send.at[place],
                recv_sem=gather_recv.at[place],
                device_id=(lax.rem(gx + i, GX), gy),
                device_id_type=MESH,
            ).start()
            return carry

        lax.fori_loop(1, GX, send, 0)

    def spread_gy(buf, place):
        def send(i, carry):
            pltpu.make_async_remote_copy(
                src_ref=buf.at[gy],
                dst_ref=buf.at[gy],
                send_sem=gather_send.at[place],
                recv_sem=gather_recv.at[place],
                device_id=(gx, lax.rem(gy + i, GY)),
                device_id_type=MESH,
            ).start()
            return carry

        lax.fori_loop(1, GY, send, 0)

    def wait_all(sem, buf, count):
        held = buf.at[pl.ds(0, count)]
        pltpu.make_async_copy(held, held, sem).wait()

    spread_gx(part_buf, 0)
    next_gx = (lax.rem(gx + 1, GX), gy)
    last_gx = (lax.rem(gx + GX - 1, GX), gy)
    next_gy = (gx, lax.rem(gy + 1, GY))
    last_gy = (gx, lax.rem(gy + GY - 1, GY))
    half = BORDER * RANK
    halos = []
    for place, (src, dst, device) in enumerate(
        (
            (points_v.at[:, pl.ds(half, half)], points_halo.at[0], next_gy),
            (points_v.at[:, pl.ds(0, half)], points_halo.at[1], last_gy),
            (coef, coef_halo.at[0], next_gx),
            (coef, coef_halo.at[1], last_gx),
        )
    ):
        halos.append(
            pltpu.make_async_remote_copy(
                src_ref=src,
                dst_ref=dst,
                send_sem=halo_send.at[place],
                recv_sem=halo_recv.at[place],
                device_id=device,
                device_id_type=MESH,
            )
        )
        halos[-1].start()
    spread_gy(root_buf, 1)

    load_pc.wait()
    for pair in range(GX // 2):
        blocks = []
        for q in (2 * pair, 2 * pair + 1):
            far = (jnp.abs(gx - q) >= 2).astype(F32).astype(BF)
            blocks.append(pc_v[q] * far)
        pc_cat[:, 128 * pair : 128 * pair + 128] = jnp.concatenate(blocks, axis=1)
    load_kind.wait()
    zero_block = jnp.zeros((RANK, RANK), BF)
    for t in range(KINDS):
        kind_left[t] = jnp.concatenate([kind_v[t], zero_block], axis=1)
        kind_right[t] = jnp.concatenate([zero_block, kind_v[t]], axis=1)
    load_rc.wait()
    for pair in range(ROOT_SLOTS // 2):
        rc_cat[:, 128 * pair : 128 * pair + 128] = jnp.concatenate(
            [rc_v[2 * pair], rc_v[2 * pair + 1]], axis=1
        )

    def expand(x, left, right, place):
        turned = jnp.concatenate([x[:, RANK:], x[:, :RANK]], axis=1)
        left[place] = x * left_mask
        right[place + 1] = x * right_mask
        left[place + 1] = turned * left_mask
        right[place] = turned * right_mask

    for pair in range(LEAVES // 2):
        expand(points_v[:, 128 * pair : 128 * pair + 128], near_left, near_right, BORDER + 2 * pair)
    window = 2 * LEAVES
    near_left[window] = jnp.zeros((RHS, 128), BF)
    near_right[window] = jnp.zeros((RHS, 128), BF)

    wait_all(gather_recv.at[0], part_buf, GX - 1)
    lhs = [
        part_buf[2 * pair] * left_mask + part_buf[2 * pair + 1] * right_mask
        for pair in range(GX // 2)
    ]
    plane = dot_nt(jnp.concatenate(lhs, axis=1), pc_cat[...])
    high = plane.astype(BF).astype(F32)
    sum_buf[gy] = jnp.concatenate([high, plane - high], axis=1).astype(BF)
    spread_gy(sum_buf, 2)

    halos[0].wait_recv()
    halos[1].wait_recv()
    for side in range(2):
        for pair in range(BORDER // 2):
            expand(
                points_halo[side, :, 128 * pair : 128 * pair + 128],
                near_left,
                near_right,
                side * (BORDER + LEAVES) + 2 * pair,
            )
    load_near.wait()
    load_near_source.wait()
    load_near_count.wait()
    for c in range(CHUNKS):
        rows = []
        for leaf in range(4 * c, 4 * c + 4):
            count = near_count[leaf]
            places = []
            for slot in range(NEAR):
                place = near_source[slot, leaf] - first_leaf + BORDER
                place = jnp.minimum(jnp.maximum(place, 0), window - 1)
                places.append(jnp.where(slot < count, place, window))
            rows.append(
                jnp.concatenate(
                    [
                        near_left[places[0]] + near_right[places[1]],
                        near_left[places[2]] + near_right[places[3]],
                    ],
                    axis=1,
                )
            )
        full = dot_nt(jnp.concatenate(rows, axis=0), near_v[4 * c : 4 * c + 4].reshape(256, 256))
        near_rows[:, 256 * c : 256 * c + 256] = diagonal(full)

    halos[2].wait_recv()
    halos[3].wait_recv()
    for side in range(2):
        for pair in range(LEAVES // 2):
            expand(
                coef_halo[side, :, 128 * pair : 128 * pair + 128],
                far_left,
                far_right,
                side * LEAVES + 2 * pair,
            )
    load_far_source.wait()
    load_far_kind.wait()
    for c in range(CHUNKS):
        rows = []
        matrices = []
        for leaf in range(4 * c, 4 * c + 4):
            places = []
            kinds = []
            for slot in range(FAR):
                source = far_source[slot, leaf] - first_leaf
                place = jnp.where(
                    source < 0, source + GY * LEAVES, source - GY * LEAVES + LEAVES
                )
                places.append(jnp.minimum(jnp.maximum(place, 0), window - 1))
                kinds.append(far_kind[slot, leaf])
            rows.append(
                jnp.concatenate(
                    [
                        far_left[places[0]] + far_right[places[1]],
                        far_left[places[2]] + far_right[places[3]],
                    ],
                    axis=1,
                )
            )
            matrices.append(
                jnp.concatenate(
                    [
                        kind_left[kinds[0]] + kind_right[kinds[1]],
                        kind_left[kinds[2]] + kind_right[kinds[3]],
                    ],
                    axis=1,
                )
            )
        full = dot_nt(jnp.concatenate(rows, axis=0), jnp.concatenate(matrices, axis=0))
        far_rows[:, 256 * c : 256 * c + 256] = diagonal(full)

    wait_all(gather_recv.at[1], root_buf, GY - 1)
    load_root_source.wait()
    chosen = [
        root_buf[root_source[0, 2 * pair]] * left_mask
        + root_buf[root_source[0, 2 * pair + 1]] * right_mask
        for pair in range(ROOT_SLOTS // 2)
    ]
    beside = dot_nt(jnp.concatenate(chosen, axis=1), rc_cat[...])
    beside = jnp.where(root_keep, beside, 0.0).astype(BF)

    load_row.wait()
    load_down.wait()
    load_pd.wait()
    unit = (
        lax.broadcasted_iota(jnp.int32, (RANK, RANK), 0)
        == lax.broadcasted_iota(jnp.int32, (RANK, RANK), 1)
    )
    plane_turned = dot_nt(unit.astype(F32).astype(BF), pd_v[...])
    keep_root = lax.broadcasted_iota(jnp.int32, (RANK, RANK), 1) < root_rank[0]
    plane_turned = jnp.where(keep_root, plane_turned, 0.0).astype(BF)
    downward = jnp.concatenate([beside, plane_turned], axis=0)
    for c in range(CHUNKS):
        span = slice(256 * c, 256 * c + 256)
        leaf_out = dot_nt(downward, down_v[4 * c : 4 * c + 4].reshape(256, RANK))
        leaf_out = jnp.concatenate(
            [leaf_out[:RHS] + far_rows[:, span], leaf_out[RHS:]], axis=0
        )
        keep = jnp.concatenate([keep_lanes[:, span]] * 10, axis=0)
        leaf_out = jnp.where(keep > 0.0, leaf_out, 0.0).astype(BF)
        values = dot_nn(leaf_out, block_diag(row_v[:, span]))
        near_rows[:, span] += values[:RHS]
        plane_map[:, span] = values[RHS:].astype(BF)

    wait_all(gather_recv.at[2], sum_buf, GY - 1)
    total = [sum_buf[q].astype(F32) for q in range(GY)]
    while len(total) > 1:
        total = [a + b for a, b in zip(total[0::2], total[1::2])]
    plane_out = (total[0][:, :RANK] + total[0][:, RANK:]).astype(BF)
    for c in range(CHUNKS):
        span = slice(256 * c, 256 * c + 256)
        out[:, span] = (near_rows[:, span] + dot_nn(plane_out, plane_map[:, span])).astype(BF)

    for halo in halos:
        halo.wait_send()
    wait_all(gather_send.at[0], part_buf, GX - 1)
    wait_all(gather_send.at[1], root_buf, GY - 1)
    wait_all(gather_send.at[2], sum_buf, GY - 1)


def per_device(
    points_in,
    near_blocks,
    near_source,
    near_count,
    col_basis,
    row_basis,
    up_transfer,
    down_transfer,
    leaf_rank,
    kind_table,
    far_source,
    far_kind,
    root_rank,
    root_coupling,
    root_source,
    plane_up,
    plane_down,
    plane_coupling,
):
    hbm = pl.BlockSpec(memory_space=pltpu.HBM)
    return pl.pallas_call(
        kernel,
        out_shape=jax.ShapeDtypeStruct((RHS, SPAN), BF),
        in_specs=[hbm] * 16 + [pl.BlockSpec(memory_space=pltpu.SMEM), hbm],
        out_specs=pl.BlockSpec(memory_space=pltpu.VMEM),
        scratch_shapes=[
            pltpu.SMEM((NEAR, LEAVES), jnp.int32),
            pltpu.SMEM((LEAVES,), jnp.int32),
            pltpu.SMEM((LEAVES,), jnp.int32),
            pltpu.SMEM((FAR, LEAVES), jnp.int32),
            pltpu.SMEM((FAR, LEAVES), jnp.int32),
            pltpu.SMEM((1, ROOT_SLOTS), jnp.int32),
            pltpu.VMEM((RHS, SPAN), BF),
            pltpu.VMEM((RANK, SPAN), BF),
            pltpu.VMEM((LEAVES, RANK, RANK), BF),
            pltpu.VMEM((RANK, RANK), BF),
            pltpu.VMEM((GX, RANK, RANK), BF),
            pltpu.VMEM((LEAVES, RANK, NEAR * RANK), BF),
            pltpu.VMEM((KINDS, RANK, RANK), BF),
            pltpu.VMEM((RANK, SPAN), BF),
            pltpu.VMEM((ROOT_SLOTS, RANK, RANK), BF),
            pltpu.VMEM((LEAVES, RANK, RANK), BF),
            pltpu.VMEM((RANK, RANK), BF),
            pltpu.VMEM((2, RHS, BORDER * RANK), BF),
            pltpu.VMEM((RHS, SPAN), BF),
            pltpu.VMEM((2, RHS, SPAN), BF),
            pltpu.VMEM((GX, RHS, 128), BF),
            pltpu.VMEM((GY, RHS, 128), BF),
            pltpu.VMEM((GY, RHS, 128), BF),
            pltpu.VMEM((2 * LEAVES + 1, RHS, 128), BF),
            pltpu.VMEM((2 * LEAVES + 1, RHS, 128), BF),
            pltpu.VMEM((2 * LEAVES, RHS, 128), BF),
            pltpu.VMEM((2 * LEAVES, RHS, 128), BF),
            pltpu.VMEM((KINDS, RANK, 128), BF),
            pltpu.VMEM((KINDS, RANK, 128), BF),
            pltpu.VMEM((RANK, GX * RANK), BF),
            pltpu.VMEM((RANK, ROOT_SLOTS * RANK), BF),
            pltpu.VMEM((RANK, SPAN), BF),
            pltpu.VMEM((8, SPAN), F32),
            pltpu.VMEM((RHS, SPAN), F32),
            pltpu.VMEM((RHS, SPAN), F32),
            pltpu.SemaphoreType.DMA((17,)),
            pltpu.SemaphoreType.DMA((4,)),
            pltpu.SemaphoreType.DMA((4,)),
            pltpu.SemaphoreType.DMA((3,)),
            pltpu.SemaphoreType.DMA((3,)),
        ],
        compiler_params=pltpu.CompilerParams(
            collective_id=0, has_side_effects=True, vmem_limit_bytes=32 * 2**20
        ),
        name="h2_product",
    )(
        *(
            array if array.size == 1 else pltpu.with_memory_space_constraint(array, pltpu.HBM)
            for array in (
                points_in,
                col_basis,
                up_transfer,
                plane_up,
                plane_coupling,
                near_blocks,
                kind_table,
                row_basis,
                root_coupling,
                down_transfer,
                plane_down,
                near_source.T,
                near_count,
                leaf_rank,
                far_source.T,
                far_kind.T,
                root_rank,
                root_source,
            )
        )
    )


def solution(mesh):
    return jax.shard_map(
        per_device,
        mesh=mesh,
        in_specs=(
            P(None, ("gx", "gy")),
            P(("gx", "gy"), None, None),
            P(("gx", "gy"), None),
            P(("gx", "gy")),
            P(None, ("gx", "gy")),
            P(None, ("gx", "gy")),
            P(("gx", "gy"), None, None),
            P(("gx", "gy"), None, None),
            P(("gx", "gy")),
            P(),
            P(("gx", "gy"), None),
            P(("gx", "gy"), None),
            P(("gx", "gy")),
            P(("gx", "gy"), None, None, None),
            P(("gx", "gy"), None),
            P(("gx", "gy"), None, None),
            P(("gx", "gy"), None, None),
            P("gx", None, None, None),
        ),
        out_specs=P(None, ("gx", "gy")),
        check_vma=False,
    )
```

```python
import jax
import jax.numpy as jnp
from jax import lax
from jax.experimental import pallas as pl
from jax.experimental.pallas import tpu as pltpu
from jax.sharding import PartitionSpec as P

MESH = pl.DeviceIdType.MESH
BF = jnp.bfloat16
F32 = jnp.float32

RHS = 16
LEAVES = 32
RANK = 64
BORDER = 16
GX = 16
GY = 32
NEAR = 4
FAR = 4
KINDS = 16
ROOT_SLOTS = 8
CHUNKS = 8
SPAN = LEAVES * RANK


def dot_nt(a, b):
    return lax.dot_general(a, b, (((1,), (1,)), ((), ())), preferred_element_type=F32)


def dot_nn(a, b):
    return lax.dot_general(a, b, (((1,), (0,)), ((), ())), preferred_element_type=F32)


def kernel(
    points,
    col,
    up,
    plane_up,
    plane_coupling,
    near_blocks,
    kind_table,
    row,
    root_coupling,
    down,
    plane_down,
    near_source_h,
    near_count_h,
    leaf_rank_h,
    far_source_h,
    far_kind_h,
    root_rank,
    root_source_h,
    out,
    near_source,
    near_count,
    leaf_rank,
    far_source,
    far_kind,
    root_source,
    points_v,
    col_v,
    up_v,
    pu_v,
    pc_v,
    near_v,
    kind_v,
    row_v,
    rc_v,
    down_v,
    pd_v,
    points_halo,
    coef,
    coef_halo,
    part_buf,
    root_buf,
    sum_buf,
    near_left,
    near_right,
    far_left,
    far_right,
    kind_left,
    kind_right,
    pc_cat,
    rc_cat,
    plane_map,
    keep_lanes,
    far_rows,
    near_rows,
    load_sem,
    halo_send,
    halo_recv,
    gather_send,
    gather_recv,
):
    gx = lax.axis_index("gx")
    gy = lax.axis_index("gy")
    first_leaf = (gx * GY + gy) * LEAVES

    pairs = (
        (leaf_rank_h, leaf_rank),
        (points, points_v),
        (col, col_v),
        (up, up_v),
        (plane_up.at[0], pu_v),
        (plane_coupling.at[0], pc_v),
        (near_source_h, near_source),
        (near_count_h, near_count),
        (near_blocks, near_v),
        (kind_table, kind_v),
        (row, row_v),
        (root_coupling.at[0], rc_v),
        (down, down_v),
        (plane_down.at[0], pd_v),
        (far_source_h, far_source),
        (far_kind_h, far_kind),
        (root_source_h, root_source),
    )
    loads = [
        pltpu.make_async_copy(src, dst, load_sem.at[place])
        for place, (src, dst) in enumerate(pairs)
    ]
    (
        load_leaf_rank,
        load_points,
        load_col,
        load_up,
        load_pu,
        load_pc,
        load_near_source,
        load_near_count,
        load_near,
        load_kind,
        load_row,
        load_rc,
        load_down,
        load_pd,
        load_far_source,
        load_far_kind,
        load_root_source,
    ) = loads
    for load in loads[:5]:
        load.start()

    barrier = pltpu.get_barrier_semaphore()

    def greet_gx(i, carry):
        pl.semaphore_signal(
            barrier, inc=1, device_id=((gx + i) & (GX - 1), gy), device_id_type=MESH
        )
        return carry

    def greet_gy(i, carry):
        pl.semaphore_signal(
            barrier, inc=1, device_id=(gx, (gy + i) & (GY - 1)), device_id_type=MESH
        )
        return carry

    lax.fori_loop(1, GX, greet_gx, 0)
    lax.fori_loop(1, GY, greet_gy, 0)

    lane = lax.broadcasted_iota(jnp.int32, (RHS, 128), 1)
    low = lane < RANK
    left_mask = low.astype(F32).astype(BF)
    right_mask = (lane >= RANK).astype(F32).astype(BF)
    lane_leaf = lax.broadcasted_iota(jnp.int32, (RANK, 256), 1) // RANK
    leaf_masks = [(lane_leaf == i).astype(F32).astype(BF) for i in range(4)]

    def block_diag(block):
        return jnp.concatenate([block * mask for mask in leaf_masks], axis=0)

    def diagonal(full):
        first = jnp.where(low, full[0:16, 0:128], full[16:32, 0:128])
        second = jnp.where(low, full[32:48, 128:256], full[48:64, 128:256])
        return jnp.concatenate([first, second], axis=1)

    lane_rank = lax.broadcasted_iota(jnp.int32, (8, 128), 1)
    in_low = lane_rank < RANK
    rank_of_lane = jnp.where(in_low, lane_rank, lane_rank - RANK)
    load_leaf_rank.wait()
    for pair in range(LEAVES // 2):
        ranks = jnp.where(in_low, leaf_rank[2 * pair], leaf_rank[2 * pair + 1])
        keep_lanes[:, 128 * pair : 128 * pair + 128] = (rank_of_lane < ranks).astype(F32)

    load_points.wait()
    load_col.wait()
    for c in range(CHUNKS):
        span = slice(256 * c, 256 * c + 256)
        full = dot_nt(points_v[:, span], block_diag(col_v[:, span]))
        keep = jnp.concatenate([keep_lanes[:, span]] * 2, axis=0)
        coef[:, span] = jnp.where(keep > 0.0, full, 0.0).astype(BF)

    load_up.wait()
    load_pu.wait()
    for load in loads[5:]:
        load.start()
    root = jnp.zeros((RHS, RANK), F32)
    for c in range(CHUNKS):
        root = root + dot_nn(
            coef[:, 256 * c : 256 * c + 256], up_v[4 * c : 4 * c + 4].reshape(256, RANK)
        )
    root_keep = lax.broadcasted_iota(jnp.int32, (RHS, RANK), 1) < root_rank[0]
    root = jnp.where(root_keep, root, 0.0)
    part = dot_nn(root.astype(BF), pu_v[...])
    part_buf[gx] = jnp.concatenate([part, part], axis=1).astype(BF)
    root_buf[gy] = jnp.concatenate([root, root], axis=1).astype(BF)

    pl.semaphore_wait(barrier, GX - 1 + GY - 1)

    def spread_gx(buf, place):
        def send(i, carry):
            peer = i + ((i - gx + GX) >> 4)
            pltpu.make_async_remote_copy(
                src_ref=buf.at[gx],
                dst_ref=buf.at[gx],
                send_sem=gather_send.at[place],
                recv_sem=gather_recv.at[place],
                device_id=(peer, gy),
                device_id_type=MESH,
            ).start()
            return carry

        lax.fori_loop(0, GX - 1, send, 0)

    def spread_gy(buf, place):
        def send(i, carry):
            peer = i + ((i - gy + GY) >> 5)
            pltpu.make_async_remote_copy(
                src_ref=buf.at[gy],
                dst_ref=buf.at[gy],
                send_sem=gather_send.at[place],
                recv_sem=gather_recv.at[place],
                device_id=(gx, peer),
                device_id_type=MESH,
            ).start()
            return carry

        lax.fori_loop(0, GY - 1, send, 0)

    def wait_all(sem, buf, count):
        held = buf.at[pl.ds(0, count)]
        pltpu.make_async_copy(held, held, sem).wait()

    spread_gx(part_buf, 0)
    next_gx = ((gx + 1) & (GX - 1), gy)
    last_gx = ((gx - 1) & (GX - 1), gy)
    next_gy = (gx, (gy + 1) & (GY - 1))
    last_gy = (gx, (gy - 1) & (GY - 1))
    half = BORDER * RANK
    halos = []
    for place, (src, dst, device) in enumerate(
        (
            (points_v.at[:, pl.ds(half, half)], points_halo.at[0], next_gy),
            (points_v.at[:, pl.ds(0, half)], points_halo.at[1], last_gy),
            (coef, coef_halo.at[0], next_gx),
            (coef, coef_halo.at[1], last_gx),
        )
    ):
        halos.append(
            pltpu.make_async_remote_copy(
                src_ref=src,
                dst_ref=dst,
                send_sem=halo_send.at[place],
                recv_sem=halo_recv.at[place],
                device_id=device,
                device_id_type=MESH,
            )
        )
        halos[-1].start()
    spread_gy(root_buf, 1)

    load_pc.wait()
    for pair in range(GX // 2):
        blocks = []
        for q in (2 * pair, 2 * pair + 1):
            far = (jnp.abs(gx - q) >= 2).astype(F32).astype(BF)
            blocks.append(pc_v[q] * far)
        pc_cat[:, 128 * pair : 128 * pair + 128] = jnp.concatenate(blocks, axis=1)
    load_kind.wait()
    zero_block = jnp.zeros((RANK, RANK), BF)
    for t in range(KINDS):
        kind_left[t] = jnp.concatenate([kind_v[t], zero_block], axis=1)
        kind_right[t] = jnp.concatenate([zero_block, kind_v[t]], axis=1)
    load_rc.wait()
    for pair in range(ROOT_SLOTS // 2):
        rc_cat[:, 128 * pair : 128 * pair + 128] = jnp.concatenate(
            [rc_v[2 * pair], rc_v[2 * pair + 1]], axis=1
        )

    def expand(x, left, right, place):
        turned = jnp.concatenate([x[:, RANK:], x[:, :RANK]], axis=1)
        left[place] = x * left_mask
        right[place + 1] = x * right_mask
        left[place + 1] = turned * left_mask
        right[place] = turned * right_mask

    for pair in range(LEAVES // 2):
        expand(points_v[:, 128 * pair : 128 * pair + 128], near_left, near_right, BORDER + 2 * pair)
    window = 2 * LEAVES
    near_left[window] = jnp.zeros((RHS, 128), BF)
    near_right[window] = jnp.zeros((RHS, 128), BF)

    wait_all(gather_recv.at[0], part_buf, GX - 1)
    lhs = [
        part_buf[2 * pair] * left_mask + part_buf[2 * pair + 1] * right_mask
        for pair in range(GX // 2)
    ]
    plane = dot_nt(jnp.concatenate(lhs, axis=1), pc_cat[...])
    high = plane.astype(BF).astype(F32)
    sum_buf[gy] = jnp.concatenate([high, plane - high], axis=1).astype(BF)
    spread_gy(sum_buf, 2)

    halos[0].wait_recv()
    halos[1].wait_recv()
    for side in range(2):
        for pair in range(BORDER // 2):
            expand(
                points_halo[side, :, 128 * pair : 128 * pair + 128],
                near_left,
                near_right,
                side * (BORDER + LEAVES) + 2 * pair,
            )
    load_near.wait()
    load_near_source.wait()
    load_near_count.wait()
    for c in range(CHUNKS):
        rows = []
        for leaf in range(4 * c, 4 * c + 4):
            count = near_count[leaf]
            places = []
            for slot in range(NEAR):
                place = near_source[slot, leaf] - first_leaf + BORDER
                place = jnp.minimum(jnp.maximum(place, 0), window - 1)
                places.append(jnp.where(slot < count, place, window))
            rows.append(
                jnp.concatenate(
                    [
                        near_left[places[0]] + near_right[places[1]],
                        near_left[places[2]] + near_right[places[3]],
                    ],
                    axis=1,
                )
            )
        full = dot_nt(jnp.concatenate(rows, axis=0), near_v[4 * c : 4 * c + 4].reshape(256, 256))
        near_rows[:, 256 * c : 256 * c + 256] = diagonal(full)

    halos[2].wait_recv()
    halos[3].wait_recv()
    for side in range(2):
        for pair in range(LEAVES // 2):
            expand(
                coef_halo[side, :, 128 * pair : 128 * pair + 128],
                far_left,
                far_right,
                side * LEAVES + 2 * pair,
            )
    load_far_source.wait()
    load_far_kind.wait()
    for c in range(CHUNKS):
        rows = []
        matrices = []
        for leaf in range(4 * c, 4 * c + 4):
            places = []
            kinds = []
            for slot in range(FAR):
                source = far_source[slot, leaf] - first_leaf
                place = jnp.where(
                    source < 0, source + GY * LEAVES, source - GY * LEAVES + LEAVES
                )
                places.append(jnp.minimum(jnp.maximum(place, 0), window - 1))
                kinds.append(far_kind[slot, leaf])
            rows.append(
                jnp.concatenate(
                    [
                        far_left[places[0]] + far_right[places[1]],
                        far_left[places[2]] + far_right[places[3]],
                    ],
                    axis=1,
                )
            )
            matrices.append(
                jnp.concatenate(
                    [
                        kind_left[kinds[0]] + kind_right[kinds[1]],
                        kind_left[kinds[2]] + kind_right[kinds[3]],
                    ],
                    axis=1,
                )
            )
        full = dot_nt(jnp.concatenate(rows, axis=0), jnp.concatenate(matrices, axis=0))
        far_rows[:, 256 * c : 256 * c + 256] = diagonal(full)

    wait_all(gather_recv.at[1], root_buf, GY - 1)
    load_root_source.wait()
    chosen = [
        root_buf[root_source[0, 2 * pair]] * left_mask
        + root_buf[root_source[0, 2 * pair + 1]] * right_mask
        for pair in range(ROOT_SLOTS // 2)
    ]
    beside = dot_nt(jnp.concatenate(chosen, axis=1), rc_cat[...])
    beside = jnp.where(root_keep, beside, 0.0).astype(BF)

    load_row.wait()
    load_down.wait()
    load_pd.wait()
    unit = (
        lax.broadcasted_iota(jnp.int32, (RANK, RANK), 0)
        == lax.broadcasted_iota(jnp.int32, (RANK, RANK), 1)
    )
    plane_turned = dot_nt(unit.astype(F32).astype(BF), pd_v[...])
    keep_root = lax.broadcasted_iota(jnp.int32, (RANK, RANK), 1) < root_rank[0]
    plane_turned = jnp.where(keep_root, plane_turned, 0.0).astype(BF)
    downward = jnp.concatenate([beside, plane_turned], axis=0)
    for c in range(CHUNKS):
        span = slice(256 * c, 256 * c + 256)
        leaf_out = dot_nt(downward, down_v[4 * c : 4 * c + 4].reshape(256, RANK))
        leaf_out = jnp.concatenate(
            [leaf_out[:RHS] + far_rows[:, span], leaf_out[RHS:]], axis=0
        )
        keep = jnp.concatenate([keep_lanes[:, span]] * 10, axis=0)
        leaf_out = jnp.where(keep > 0.0, leaf_out, 0.0).astype(BF)
        values = dot_nn(leaf_out, block_diag(row_v[:, span]))
        near_rows[:, span] += values[:RHS]
        plane_map[:, span] = values[RHS:].astype(BF)

    wait_all(gather_recv.at[2], sum_buf, GY - 1)
    total = [sum_buf[q].astype(F32) for q in range(GY)]
    while len(total) > 1:
        total = [a + b for a, b in zip(total[0::2], total[1::2])]
    plane_out = (total[0][:, :RANK] + total[0][:, RANK:]).astype(BF)
    for c in range(CHUNKS):
        span = slice(256 * c, 256 * c + 256)
        out[:, span] = (near_rows[:, span] + dot_nn(plane_out, plane_map[:, span])).astype(BF)

    for halo in halos:
        halo.wait_send()
    wait_all(gather_send.at[0], part_buf, GX - 1)
    wait_all(gather_send.at[1], root_buf, GY - 1)
    wait_all(gather_send.at[2], sum_buf, GY - 1)


def per_device(
    points_in,
    near_blocks,
    near_source,
    near_count,
    col_basis,
    row_basis,
    up_transfer,
    down_transfer,
    leaf_rank,
    kind_table,
    far_source,
    far_kind,
    root_rank,
    root_coupling,
    root_source,
    plane_up,
    plane_down,
    plane_coupling,
):
    hbm = pl.BlockSpec(memory_space=pltpu.HBM)
    return pl.pallas_call(
        kernel,
        out_shape=jax.ShapeDtypeStruct((RHS, SPAN), BF),
        in_specs=[hbm] * 16 + [pl.BlockSpec(memory_space=pltpu.SMEM), hbm],
        out_specs=pl.BlockSpec(memory_space=pltpu.VMEM),
        scratch_shapes=[
            pltpu.SMEM((NEAR, LEAVES), jnp.int32),
            pltpu.SMEM((LEAVES,), jnp.int32),
            pltpu.SMEM((LEAVES,), jnp.int32),
            pltpu.SMEM((FAR, LEAVES), jnp.int32),
            pltpu.SMEM((FAR, LEAVES), jnp.int32),
            pltpu.SMEM((1, ROOT_SLOTS), jnp.int32),
            pltpu.VMEM((RHS, SPAN), BF),
            pltpu.VMEM((RANK, SPAN), BF),
            pltpu.VMEM((LEAVES, RANK, RANK), BF),
            pltpu.VMEM((RANK, RANK), BF),
            pltpu.VMEM((GX, RANK, RANK), BF),
            pltpu.VMEM((LEAVES, RANK, NEAR * RANK), BF),
            pltpu.VMEM((KINDS, RANK, RANK), BF),
            pltpu.VMEM((RANK, SPAN), BF),
            pltpu.VMEM((ROOT_SLOTS, RANK, RANK), BF),
            pltpu.VMEM((LEAVES, RANK, RANK), BF),
            pltpu.VMEM((RANK, RANK), BF),
            pltpu.VMEM((2, RHS, BORDER * RANK), BF),
            pltpu.VMEM((RHS, SPAN), BF),
            pltpu.VMEM((2, RHS, SPAN), BF),
            pltpu.VMEM((GX, RHS, 128), BF),
            pltpu.VMEM((GY, RHS, 128), BF),
            pltpu.VMEM((GY, RHS, 128), BF),
            pltpu.VMEM((2 * LEAVES + 1, RHS, 128), BF),
            pltpu.VMEM((2 * LEAVES + 1, RHS, 128), BF),
            pltpu.VMEM((2 * LEAVES, RHS, 128), BF),
            pltpu.VMEM((2 * LEAVES, RHS, 128), BF),
            pltpu.VMEM((KINDS, RANK, 128), BF),
            pltpu.VMEM((KINDS, RANK, 128), BF),
            pltpu.VMEM((RANK, GX * RANK), BF),
            pltpu.VMEM((RANK, ROOT_SLOTS * RANK), BF),
            pltpu.VMEM((RANK, SPAN), BF),
            pltpu.VMEM((8, SPAN), F32),
            pltpu.VMEM((RHS, SPAN), F32),
            pltpu.VMEM((RHS, SPAN), F32),
            pltpu.SemaphoreType.DMA((17,)),
            pltpu.SemaphoreType.DMA((4,)),
            pltpu.SemaphoreType.DMA((4,)),
            pltpu.SemaphoreType.DMA((3,)),
            pltpu.SemaphoreType.DMA((3,)),
        ],
        compiler_params=pltpu.CompilerParams(
            collective_id=0, has_side_effects=True, vmem_limit_bytes=32 * 2**20
        ),
        name="h2_product",
    )(
        *(
            array if array.size == 1 else pltpu.with_memory_space_constraint(array, pltpu.HBM)
            for array in (
                points_in,
                col_basis,
                up_transfer,
                plane_up,
                plane_coupling,
                near_blocks,
                kind_table,
                row_basis,
                root_coupling,
                down_transfer,
                plane_down,
                near_source.T,
                near_count,
                leaf_rank,
                far_source.T,
                far_kind.T,
                root_rank,
                root_source,
            )
        )
    )


def solution(mesh):
    return jax.shard_map(
        per_device,
        mesh=mesh,
        in_specs=(
            P(None, ("gx", "gy")),
            P(("gx", "gy"), None, None),
            P(("gx", "gy"), None),
            P(("gx", "gy")),
            P(None, ("gx", "gy")),
            P(None, ("gx", "gy")),
            P(("gx", "gy"), None, None),
            P(("gx", "gy"), None, None),
            P(("gx", "gy")),
            P(),
            P(("gx", "gy"), None),
            P(("gx", "gy"), None),
            P(("gx", "gy")),
            P(("gx", "gy"), None, None, None),
            P(("gx", "gy"), None),
            P(("gx", "gy"), None, None),
            P(("gx", "gy"), None, None),
            P("gx", None, None, None),
        ),
        out_specs=P(None, ("gx", "gy")),
        check_vma=False,
    )
```

```python
import jax
import jax.numpy as jnp
from jax import lax
from jax.experimental import pallas as pl
from jax.experimental.pallas import tpu as pltpu
from jax.sharding import PartitionSpec as P

MESH = pl.DeviceIdType.MESH
BF = jnp.bfloat16
F32 = jnp.float32

RHS = 16
LEAVES = 32
RANK = 64
BORDER = 16
GX = 16
GY = 32
NEAR = 4
FAR = 4
KINDS = 16
ROOT_SLOTS = 8
CHUNKS = 8
SPAN = LEAVES * RANK


def dot_nt(a, b):
    return lax.dot_general(a, b, (((1,), (1,)), ((), ())), preferred_element_type=F32)


def dot_nn(a, b):
    return lax.dot_general(a, b, (((1,), (0,)), ((), ())), preferred_element_type=F32)


def kernel(
    points,
    col,
    up,
    plane_up,
    plane_coupling,
    near_blocks,
    kind_table,
    row,
    root_coupling,
    down,
    plane_down,
    near_source_h,
    near_count_h,
    leaf_rank_h,
    far_source_h,
    far_kind_h,
    root_rank,
    root_source_h,
    out,
    near_source,
    near_count,
    leaf_rank,
    far_source,
    far_kind,
    root_source,
    points_v,
    col_v,
    up_v,
    pu_v,
    pc_v,
    near_v,
    kind_v,
    row_v,
    rc_v,
    down_v,
    pd_v,
    points_halo,
    coef,
    coef_halo,
    part_buf,
    root_buf,
    sum_buf,
    near_left,
    near_right,
    far_left,
    far_right,
    kind_left,
    kind_right,
    pc_cat,
    rc_cat,
    plane_map,
    keep_lanes,
    far_rows,
    near_rows,
    load_sem,
    halo_send,
    halo_recv,
    gather_send,
    gather_recv,
    part_recv,
):
    gx = lax.axis_index("gx")
    gy = lax.axis_index("gy")
    first_leaf = (gx * GY + gy) * LEAVES

    pairs = (
        (leaf_rank_h, leaf_rank),
        (points, points_v),
        (col, col_v),
        (up, up_v),
        (plane_up.at[0], pu_v),
        (plane_coupling.at[0], pc_v),
        (near_source_h, near_source),
        (near_count_h, near_count),
        (near_blocks, near_v),
        (kind_table, kind_v),
        (row, row_v),
        (root_coupling.at[0], rc_v),
        (down, down_v),
        (plane_down.at[0], pd_v),
        (far_source_h, far_source),
        (far_kind_h, far_kind),
        (root_source_h, root_source),
    )
    loads = [
        pltpu.make_async_copy(src, dst, load_sem.at[place])
        for place, (src, dst) in enumerate(pairs)
    ]
    (
        load_leaf_rank,
        load_points,
        load_col,
        load_up,
        load_pu,
        load_pc,
        load_near_source,
        load_near_count,
        load_near,
        load_kind,
        load_row,
        load_rc,
        load_down,
        load_pd,
        load_far_source,
        load_far_kind,
        load_root_source,
    ) = loads
    for load in loads[:5]:
        load.start()

    barrier = pltpu.get_barrier_semaphore()

    def greet_gx(i, carry):
        pl.semaphore_signal(
            barrier, inc=1, device_id=(i, gy), device_id_type=MESH
        )
        return carry

    def greet_gy(i, carry):
        pl.semaphore_signal(
            barrier, inc=1, device_id=(gx, (gy + i) & (GY - 1)), device_id_type=MESH
        )
        return carry

    lax.fori_loop(gx + 1, GX, greet_gx, 0)
    lax.fori_loop(1, GY, greet_gy, 0)

    lane = lax.broadcasted_iota(jnp.int32, (RHS, 128), 1)
    low = lane < RANK
    left_mask = low.astype(F32).astype(BF)
    right_mask = (lane >= RANK).astype(F32).astype(BF)
    lane_leaf = lax.broadcasted_iota(jnp.int32, (RANK, 256), 1) // RANK
    leaf_masks = [(lane_leaf == i).astype(F32).astype(BF) for i in range(4)]

    def block_diag(block):
        return jnp.concatenate([block * mask for mask in leaf_masks], axis=0)

    def diagonal(full):
        first = jnp.where(low, full[0:16, 0:128], full[16:32, 0:128])
        second = jnp.where(low, full[32:48, 128:256], full[48:64, 128:256])
        return jnp.concatenate([first, second], axis=1)

    lane_rank = lax.broadcasted_iota(jnp.int32, (8, 128), 1)
    in_low = lane_rank < RANK
    rank_of_lane = jnp.where(in_low, lane_rank, lane_rank - RANK)
    load_leaf_rank.wait()
    for pair in range(LEAVES // 2):
        ranks = jnp.where(in_low, leaf_rank[2 * pair], leaf_rank[2 * pair + 1])
        keep_lanes[:, 128 * pair : 128 * pair + 128] = (rank_of_lane < ranks).astype(F32)

    load_points.wait()
    load_col.wait()
    for c in range(CHUNKS):
        span = slice(256 * c, 256 * c + 256)
        full = dot_nt(points_v[:, span], block_diag(col_v[:, span]))
        keep = jnp.concatenate([keep_lanes[:, span]] * 2, axis=0)
        coef[:, span] = jnp.where(keep > 0.0, full, 0.0).astype(BF)

    load_up.wait()
    load_pu.wait()
    for load in loads[5:]:
        load.start()
    root = jnp.zeros((RHS, RANK), F32)
    for c in range(CHUNKS):
        root = root + dot_nn(
            coef[:, 256 * c : 256 * c + 256], up_v[4 * c : 4 * c + 4].reshape(256, RANK)
        )
    root_keep = lax.broadcasted_iota(jnp.int32, (RHS, RANK), 1) < root_rank[0]
    root = jnp.where(root_keep, root, 0.0)
    part = dot_nn(root.astype(BF), pu_v[...])
    part_buf[gx] = jnp.concatenate([part, part], axis=1).astype(BF)
    root_buf[gy] = jnp.concatenate([root, root], axis=1).astype(BF)

    pl.semaphore_wait(barrier, gx + GY - 1)

    def send_part(peer, carry):
        pltpu.make_async_remote_copy(
            src_ref=part_buf.at[gx],
            dst_ref=part_buf.at[gx],
            send_sem=gather_send.at[0],
            recv_sem=part_recv.at[gx],
            device_id=(peer, gy),
            device_id_type=MESH,
        ).start()
        return carry

    def wait_part(peer, carry):
        held = part_buf.at[peer]
        pltpu.make_async_copy(held, held, part_recv.at[peer]).wait()
        return carry

    def answer_part(peer, carry):
        wait_part(peer, carry)
        return send_part(peer, carry)

    def send_coef(side, device):
        return pltpu.make_async_remote_copy(
            src_ref=coef,
            dst_ref=coef_halo.at[side],
            send_sem=halo_send.at[2 + side],
            recv_sem=halo_recv.at[2 + side],
            device_id=device,
            device_id_type=MESH,
        )

    def spread_gy(buf, place):
        def send(i, carry):
            peer = i + ((i - gy + GY) >> 5)
            pltpu.make_async_remote_copy(
                src_ref=buf.at[gy],
                dst_ref=buf.at[gy],
                send_sem=gather_send.at[place],
                recv_sem=gather_recv.at[place],
                device_id=(gx, peer),
                device_id_type=MESH,
            ).start()
            return carry

        lax.fori_loop(0, GY - 1, send, 0)

    def wait_all(sem, buf, count):
        held = buf.at[pl.ds(0, count)]
        pltpu.make_async_copy(held, held, sem).wait()

    lax.fori_loop(0, gx, send_part, 0)
    next_gy = (gx, (gy + 1) & (GY - 1))
    last_gy = (gx, (gy - 1) & (GY - 1))
    half = BORDER * RANK
    halos = []
    for place, (src, dst, device) in enumerate(
        (
            (points_v.at[:, pl.ds(half, half)], points_halo.at[0], next_gy),
            (points_v.at[:, pl.ds(0, half)], points_halo.at[1], last_gy),
        )
    ):
        halos.append(
            pltpu.make_async_remote_copy(
                src_ref=src,
                dst_ref=dst,
                send_sem=halo_send.at[place],
                recv_sem=halo_recv.at[place],
                device_id=device,
                device_id_type=MESH,
            )
        )
        halos[-1].start()

    @pl.when(gx > 0)
    def _():
        send_coef(1, (gx - 1, gy)).start()

    spread_gy(root_buf, 1)

    load_pc.wait()
    for pair in range(GX // 2):
        blocks = []
        for q in (2 * pair, 2 * pair + 1):
            far = (jnp.abs(gx - q) >= 2).astype(F32).astype(BF)
            blocks.append(pc_v[q] * far)
        pc_cat[:, 128 * pair : 128 * pair + 128] = jnp.concatenate(blocks, axis=1)
    load_kind.wait()
    zero_block = jnp.zeros((RANK, RANK), BF)
    for t in range(KINDS):
        kind_left[t] = jnp.concatenate([kind_v[t], zero_block], axis=1)
        kind_right[t] = jnp.concatenate([zero_block, kind_v[t]], axis=1)
    load_rc.wait()
    for pair in range(ROOT_SLOTS // 2):
        rc_cat[:, 128 * pair : 128 * pair + 128] = jnp.concatenate(
            [rc_v[2 * pair], rc_v[2 * pair + 1]], axis=1
        )

    def expand(x, left, right, place):
        turned = jnp.concatenate([x[:, RANK:], x[:, :RANK]], axis=1)
        left[place] = x * left_mask
        right[place + 1] = x * right_mask
        left[place + 1] = turned * left_mask
        right[place] = turned * right_mask

    for pair in range(LEAVES // 2):
        expand(points_v[:, 128 * pair : 128 * pair + 128], near_left, near_right, BORDER + 2 * pair)
    window = 2 * LEAVES
    near_left[window] = jnp.zeros((RHS, 128), BF)
    near_right[window] = jnp.zeros((RHS, 128), BF)

    @pl.when(gx < GX - 1)
    def _():
        answer_part(gx + 1, 0)
        send_coef(0, (gx + 1, gy)).start()

    lax.fori_loop(gx + 2, GX, answer_part, 0)
    lax.fori_loop(0, gx, wait_part, 0)
    lhs = [
        part_buf[2 * pair] * left_mask + part_buf[2 * pair + 1] * right_mask
        for pair in range(GX // 2)
    ]
    plane = dot_nt(jnp.concatenate(lhs, axis=1), pc_cat[...])
    high = plane.astype(BF).astype(F32)
    sum_buf[gy] = jnp.concatenate([high, plane - high], axis=1).astype(BF)
    spread_gy(sum_buf, 2)

    halos[0].wait_recv()
    halos[1].wait_recv()
    for side in range(2):
        for pair in range(BORDER // 2):
            expand(
                points_halo[side, :, 128 * pair : 128 * pair + 128],
                near_left,
                near_right,
                side * (BORDER + LEAVES) + 2 * pair,
            )
    load_near.wait()
    load_near_source.wait()
    load_near_count.wait()
    for c in range(CHUNKS):
        rows = []
        for leaf in range(4 * c, 4 * c + 4):
            count = near_count[leaf]
            places = []
            for slot in range(NEAR):
                place = near_source[slot, leaf] - first_leaf + BORDER
                place = jnp.minimum(jnp.maximum(place, 0), window - 1)
                places.append(jnp.where(slot < count, place, window))
            rows.append(
                jnp.concatenate(
                    [
                        near_left[places[0]] + near_right[places[1]],
                        near_left[places[2]] + near_right[places[3]],
                    ],
                    axis=1,
                )
            )
        full = dot_nt(jnp.concatenate(rows, axis=0), near_v[4 * c : 4 * c + 4].reshape(256, 256))
        near_rows[:, 256 * c : 256 * c + 256] = diagonal(full)

    @pl.when(gx > 0)
    def _():
        send_coef(0, (gx - 1, gy)).wait_recv()

    @pl.when(gx == 0)
    def _():
        coef_halo[0] = jnp.zeros((RHS, SPAN), BF)

    @pl.when(gx < GX - 1)
    def _():
        send_coef(1, (gx + 1, gy)).wait_recv()

    @pl.when(gx == GX - 1)
    def _():
        coef_halo[1] = jnp.zeros((RHS, SPAN), BF)

    for side in range(2):
        for pair in range(LEAVES // 2):
            expand(
                coef_halo[side, :, 128 * pair : 128 * pair + 128],
                far_left,
                far_right,
                side * LEAVES + 2 * pair,
            )
    load_far_source.wait()
    load_far_kind.wait()
    for c in range(CHUNKS):
        rows = []
        matrices = []
        for leaf in range(4 * c, 4 * c + 4):
            places = []
            kinds = []
            for slot in range(FAR):
                source = far_source[slot, leaf] - first_leaf
                place = jnp.where(
                    source < 0, source + GY * LEAVES, source - GY * LEAVES + LEAVES
                )
                places.append(jnp.minimum(jnp.maximum(place, 0), window - 1))
                kinds.append(far_kind[slot, leaf])
            rows.append(
                jnp.concatenate(
                    [
                        far_left[places[0]] + far_right[places[1]],
                        far_left[places[2]] + far_right[places[3]],
                    ],
                    axis=1,
                )
            )
            matrices.append(
                jnp.concatenate(
                    [
                        kind_left[kinds[0]] + kind_right[kinds[1]],
                        kind_left[kinds[2]] + kind_right[kinds[3]],
                    ],
                    axis=1,
                )
            )
        full = dot_nt(jnp.concatenate(rows, axis=0), jnp.concatenate(matrices, axis=0))
        far_rows[:, 256 * c : 256 * c + 256] = diagonal(full)

    wait_all(gather_recv.at[1], root_buf, GY - 1)
    load_root_source.wait()
    chosen = [
        root_buf[root_source[0, 2 * pair]] * left_mask
        + root_buf[root_source[0, 2 * pair + 1]] * right_mask
        for pair in range(ROOT_SLOTS // 2)
    ]
    beside = dot_nt(jnp.concatenate(chosen, axis=1), rc_cat[...])
    beside = jnp.where(root_keep, beside, 0.0).astype(BF)

    load_row.wait()
    load_down.wait()
    load_pd.wait()
    unit = (
        lax.broadcasted_iota(jnp.int32, (RANK, RANK), 0)
        == lax.broadcasted_iota(jnp.int32, (RANK, RANK), 1)
    )
    plane_turned = dot_nt(unit.astype(F32).astype(BF), pd_v[...])
    keep_root = lax.broadcasted_iota(jnp.int32, (RANK, RANK), 1) < root_rank[0]
    plane_turned = jnp.where(keep_root, plane_turned, 0.0).astype(BF)
    downward = jnp.concatenate([beside, plane_turned], axis=0)
    for c in range(CHUNKS):
        span = slice(256 * c, 256 * c + 256)
        leaf_out = dot_nt(downward, down_v[4 * c : 4 * c + 4].reshape(256, RANK))
        leaf_out = jnp.concatenate(
            [leaf_out[:RHS] + far_rows[:, span], leaf_out[RHS:]], axis=0
        )
        keep = jnp.concatenate([keep_lanes[:, span]] * 10, axis=0)
        leaf_out = jnp.where(keep > 0.0, leaf_out, 0.0).astype(BF)
        values = dot_nn(leaf_out, block_diag(row_v[:, span]))
        near_rows[:, span] += values[:RHS]
        plane_map[:, span] = values[RHS:].astype(BF)

    wait_all(gather_recv.at[2], sum_buf, GY - 1)
    total = [sum_buf[q].astype(F32) for q in range(GY)]
    while len(total) > 1:
        total = [a + b for a, b in zip(total[0::2], total[1::2])]
    plane_out = (total[0][:, :RANK] + total[0][:, RANK:]).astype(BF)
    for c in range(CHUNKS):
        span = slice(256 * c, 256 * c + 256)
        out[:, span] = (near_rows[:, span] + dot_nn(plane_out, plane_map[:, span])).astype(BF)

    for halo in halos:
        halo.wait_send()

    @pl.when(gx > 0)
    def _():
        send_coef(1, (gx - 1, gy)).wait_send()

    @pl.when(gx < GX - 1)
    def _():
        send_coef(0, (gx + 1, gy)).wait_send()

    wait_all(gather_send.at[0], part_buf, GX - 1)
    wait_all(gather_send.at[1], root_buf, GY - 1)
    wait_all(gather_send.at[2], sum_buf, GY - 1)


def per_device(
    points_in,
    near_blocks,
    near_source,
    near_count,
    col_basis,
    row_basis,
    up_transfer,
    down_transfer,
    leaf_rank,
    kind_table,
    far_source,
    far_kind,
    root_rank,
    root_coupling,
    root_source,
    plane_up,
    plane_down,
    plane_coupling,
):
    hbm = pl.BlockSpec(memory_space=pltpu.HBM)
    return pl.pallas_call(
        kernel,
        out_shape=jax.ShapeDtypeStruct((RHS, SPAN), BF),
        in_specs=[hbm] * 16 + [pl.BlockSpec(memory_space=pltpu.SMEM), hbm],
        out_specs=pl.BlockSpec(memory_space=pltpu.VMEM),
        scratch_shapes=[
            pltpu.SMEM((NEAR, LEAVES), jnp.int32),
            pltpu.SMEM((LEAVES,), jnp.int32),
            pltpu.SMEM((LEAVES,), jnp.int32),
            pltpu.SMEM((FAR, LEAVES), jnp.int32),
            pltpu.SMEM((FAR, LEAVES), jnp.int32),
            pltpu.SMEM((1, ROOT_SLOTS), jnp.int32),
            pltpu.VMEM((RHS, SPAN), BF),
            pltpu.VMEM((RANK, SPAN), BF),
            pltpu.VMEM((LEAVES, RANK, RANK), BF),
            pltpu.VMEM((RANK, RANK), BF),
            pltpu.VMEM((GX, RANK, RANK), BF),
            pltpu.VMEM((LEAVES, RANK, NEAR * RANK), BF),
            pltpu.VMEM((KINDS, RANK, RANK), BF),
            pltpu.VMEM((RANK, SPAN), BF),
            pltpu.VMEM((ROOT_SLOTS, RANK, RANK), BF),
            pltpu.VMEM((LEAVES, RANK, RANK), BF),
            pltpu.VMEM((RANK, RANK), BF),
            pltpu.VMEM((2, RHS, BORDER * RANK), BF),
            pltpu.VMEM((RHS, SPAN), BF),
            pltpu.VMEM((2, RHS, SPAN), BF),
            pltpu.VMEM((GX, RHS, 128), BF),
            pltpu.VMEM((GY, RHS, 128), BF),
            pltpu.VMEM((GY, RHS, 128), BF),
            pltpu.VMEM((2 * LEAVES + 1, RHS, 128), BF),
            pltpu.VMEM((2 * LEAVES + 1, RHS, 128), BF),
            pltpu.VMEM((2 * LEAVES, RHS, 128), BF),
            pltpu.VMEM((2 * LEAVES, RHS, 128), BF),
            pltpu.VMEM((KINDS, RANK, 128), BF),
            pltpu.VMEM((KINDS, RANK, 128), BF),
            pltpu.VMEM((RANK, GX * RANK), BF),
            pltpu.VMEM((RANK, ROOT_SLOTS * RANK), BF),
            pltpu.VMEM((RANK, SPAN), BF),
            pltpu.VMEM((8, SPAN), F32),
            pltpu.VMEM((RHS, SPAN), F32),
            pltpu.VMEM((RHS, SPAN), F32),
            pltpu.SemaphoreType.DMA((17,)),
            pltpu.SemaphoreType.DMA((4,)),
            pltpu.SemaphoreType.DMA((4,)),
            pltpu.SemaphoreType.DMA((3,)),
            pltpu.SemaphoreType.DMA((3,)),
            pltpu.SemaphoreType.DMA((GX,)),
        ],
        compiler_params=pltpu.CompilerParams(
            collective_id=0, has_side_effects=True, vmem_limit_bytes=32 * 2**20
        ),
        name="h2_product",
    )(
        *(
            array if array.size == 1 else pltpu.with_memory_space_constraint(array, pltpu.HBM)
            for array in (
                points_in,
                col_basis,
                up_transfer,
                plane_up,
                plane_coupling,
                near_blocks,
                kind_table,
                row_basis,
                root_coupling,
                down_transfer,
                plane_down,
                near_source.T,
                near_count,
                leaf_rank,
                far_source.T,
                far_kind.T,
                root_rank,
                root_source,
            )
        )
    )


def solution(mesh):
    return jax.shard_map(
        per_device,
        mesh=mesh,
        in_specs=(
            P(None, ("gx", "gy")),
            P(("gx", "gy"), None, None),
            P(("gx", "gy"), None),
            P(("gx", "gy")),
            P(None, ("gx", "gy")),
            P(None, ("gx", "gy")),
            P(("gx", "gy"), None, None),
            P(("gx", "gy"), None, None),
            P(("gx", "gy")),
            P(),
            P(("gx", "gy"), None),
            P(("gx", "gy"), None),
            P(("gx", "gy")),
            P(("gx", "gy"), None, None, None),
            P(("gx", "gy"), None),
            P(("gx", "gy"), None, None),
            P(("gx", "gy"), None, None),
            P("gx", None, None, None),
        ),
        out_specs=P(None, ("gx", "gy")),
        check_vma=False,
    )
```

```python
import jax
import jax.numpy as jnp
from jax import lax
from jax.experimental import pallas as pl
from jax.experimental.pallas import tpu as pltpu
from jax.sharding import PartitionSpec as P

MESH = pl.DeviceIdType.MESH
BF = jnp.bfloat16
F32 = jnp.float32

RHS = 16
LEAVES = 32
RANK = 64
BORDER = 16
GX = 16
GY = 32
NEAR = 4
FAR = 4
KINDS = 16
ROOT_SLOTS = 8
CHUNKS = 8
SPAN = LEAVES * RANK


def dot_nt(a, b):
    return lax.dot_general(a, b, (((1,), (1,)), ((), ())), preferred_element_type=F32)


def dot_nn(a, b):
    return lax.dot_general(a, b, (((1,), (0,)), ((), ())), preferred_element_type=F32)


def place_of(gy):
    x, y = gy >> 3, gy & 7
    turned = jnp.where(y < 4, y, 11 - y)
    return ((turned + x) << 5) + gy


def kernel(
    points,
    col,
    up,
    plane_up,
    plane_coupling,
    near_blocks,
    kind_table,
    row,
    root_coupling,
    down,
    plane_down,
    near_source_h,
    near_count_h,
    leaf_rank_h,
    far_source_h,
    far_kind_h,
    root_rank,
    root_source_h,
    out,
    near_source,
    near_count,
    leaf_rank,
    far_source,
    far_kind,
    root_source,
    points_v,
    col_v,
    up_v,
    pu_v,
    pc_v,
    near_v,
    kind_v,
    row_v,
    rc_v,
    down_v,
    pd_v,
    points_halo,
    coef,
    coef_halo,
    part_buf,
    root_buf,
    sum_buf,
    near_left,
    near_right,
    far_left,
    far_right,
    kind_left,
    kind_right,
    pc_cat,
    rc_cat,
    plane_map,
    keep_lanes,
    far_rows,
    near_rows,
    load_sem,
    halo_send,
    halo_recv,
    gather_send,
    gather_recv,
    part_recv,
    ready,
):
    gx = lax.axis_index("gx")
    gy = lax.axis_index("gy")
    first_leaf = (gx * GY + gy) * LEAVES

    pairs = (
        (leaf_rank_h, leaf_rank),
        (points, points_v),
        (col, col_v),
        (up, up_v),
        (plane_up.at[0], pu_v),
        (plane_coupling.at[0], pc_v),
        (near_source_h, near_source),
        (near_count_h, near_count),
        (near_blocks, near_v),
        (kind_table, kind_v),
        (row, row_v),
        (root_coupling.at[0], rc_v),
        (down, down_v),
        (plane_down.at[0], pd_v),
        (far_source_h, far_source),
        (far_kind_h, far_kind),
        (root_source_h, root_source),
    )
    loads = [
        pltpu.make_async_copy(src, dst, load_sem.at[place])
        for place, (src, dst) in enumerate(pairs)
    ]
    (
        load_leaf_rank,
        load_points,
        load_col,
        load_up,
        load_pu,
        load_pc,
        load_near_source,
        load_near_count,
        load_near,
        load_kind,
        load_row,
        load_rc,
        load_down,
        load_pd,
        load_far_source,
        load_far_kind,
        load_root_source,
    ) = loads
    for load in loads[:5]:
        load.start()

    barrier = pltpu.get_barrier_semaphore()

    def greet_gx(i, carry):
        pl.semaphore_signal(
            barrier, inc=1, device_id=(i, gy), device_id_type=MESH
        )
        return carry

    my_place = place_of(gy)

    def greet_gy(i, before):
        @pl.when(place_of(i) > my_place)
        def _():
            pl.semaphore_signal(barrier, inc=1, device_id=(gx, i), device_id_type=MESH)

        return before + jnp.where(place_of(i) < my_place, 1, 0)

    def greet_gy_back(i, carry):
        @pl.when(place_of(i) < my_place)
        def _():
            pl.semaphore_signal(ready, inc=1, device_id=(gx, i), device_id_type=MESH)

        return carry

    lax.fori_loop(gx + 1, GX, greet_gx, 0)
    before = lax.fori_loop(0, GY, greet_gy, 0)

    lane = lax.broadcasted_iota(jnp.int32, (RHS, 128), 1)
    low = lane < RANK
    left_mask = low.astype(F32).astype(BF)
    right_mask = (lane >= RANK).astype(F32).astype(BF)
    lane_leaf = lax.broadcasted_iota(jnp.int32, (RANK, 256), 1) // RANK
    leaf_masks = [(lane_leaf == i).astype(F32).astype(BF) for i in range(4)]

    def block_diag(block):
        return jnp.concatenate([block * mask for mask in leaf_masks], axis=0)

    def diagonal(full):
        first = jnp.where(low, full[0:16, 0:128], full[16:32, 0:128])
        second = jnp.where(low, full[32:48, 128:256], full[48:64, 128:256])
        return jnp.concatenate([first, second], axis=1)

    lane_rank = lax.broadcasted_iota(jnp.int32, (8, 128), 1)
    in_low = lane_rank < RANK
    rank_of_lane = jnp.where(in_low, lane_rank, lane_rank - RANK)
    load_leaf_rank.wait()
    for pair in range(LEAVES // 2):
        ranks = jnp.where(in_low, leaf_rank[2 * pair], leaf_rank[2 * pair + 1])
        keep_lanes[:, 128 * pair : 128 * pair + 128] = (rank_of_lane < ranks).astype(F32)

    load_points.wait()
    load_col.wait()
    for c in range(CHUNKS):
        span = slice(256 * c, 256 * c + 256)
        full = dot_nt(points_v[:, span], block_diag(col_v[:, span]))
        keep = jnp.concatenate([keep_lanes[:, span]] * 2, axis=0)
        coef[:, span] = jnp.where(keep > 0.0, full, 0.0).astype(BF)

    load_up.wait()
    load_pu.wait()
    for load in loads[5:]:
        load.start()
    root = jnp.zeros((RHS, RANK), F32)
    for c in range(CHUNKS):
        root = root + dot_nn(
            coef[:, 256 * c : 256 * c + 256], up_v[4 * c : 4 * c + 4].reshape(256, RANK)
        )
    root_keep = lax.broadcasted_iota(jnp.int32, (RHS, RANK), 1) < root_rank[0]
    root = jnp.where(root_keep, root, 0.0)
    part = dot_nn(root.astype(BF), pu_v[...])
    part_buf[gx] = jnp.concatenate([part, part], axis=1).astype(BF)
    root_buf[gy] = jnp.concatenate([root, root], axis=1).astype(BF)

    @pl.when(gx + before > 0)
    def _():
        pl.semaphore_wait(barrier, gx + before)

    def send_part(peer, carry):
        pltpu.make_async_remote_copy(
            src_ref=part_buf.at[gx],
            dst_ref=part_buf.at[gx],
            send_sem=gather_send.at[0],
            recv_sem=part_recv.at[gx],
            device_id=(peer, gy),
            device_id_type=MESH,
        ).start()
        return carry

    def wait_part(peer, carry):
        held = part_buf.at[peer]
        pltpu.make_async_copy(held, held, part_recv.at[peer]).wait()
        return carry

    def answer_part(peer, carry):
        wait_part(peer, carry)
        return send_part(peer, carry)

    def send_coef(side, device):
        return pltpu.make_async_remote_copy(
            src_ref=coef,
            dst_ref=coef_halo.at[side],
            send_sem=halo_send.at[2 + side],
            recv_sem=halo_recv.at[2 + side],
            device_id=device,
            device_id_type=MESH,
        )

    def spread_gy(buf, place):
        def send(i, carry):
            peer = i + ((i - gy + GY) >> 5)
            pltpu.make_async_remote_copy(
                src_ref=buf.at[gy],
                dst_ref=buf.at[gy],
                send_sem=gather_send.at[place],
                recv_sem=gather_recv.at[place],
                device_id=(gx, peer),
                device_id_type=MESH,
            ).start()
            return carry

        lax.fori_loop(0, GY - 1, send, 0)

    def wait_all(sem, buf, count):
        held = buf.at[pl.ds(0, count)]
        pltpu.make_async_copy(held, held, sem).wait()

    lax.fori_loop(0, gx, send_part, 0)
    lax.fori_loop(0, GY, greet_gy_back, 0)

    @pl.when(gx > 0)
    def _():
        send_coef(1, (gx - 1, gy)).start()


    load_pc.wait()
    for pair in range(GX // 2):
        blocks = []
        for q in (2 * pair, 2 * pair + 1):
            far = (jnp.abs(gx - q) >= 2).astype(F32).astype(BF)
            blocks.append(pc_v[q] * far)
        pc_cat[:, 128 * pair : 128 * pair + 128] = jnp.concatenate(blocks, axis=1)
    load_kind.wait()
    zero_block = jnp.zeros((RANK, RANK), BF)
    for t in range(KINDS):
        kind_left[t] = jnp.concatenate([kind_v[t], zero_block], axis=1)
        kind_right[t] = jnp.concatenate([zero_block, kind_v[t]], axis=1)
    load_rc.wait()
    for pair in range(ROOT_SLOTS // 2):
        rc_cat[:, 128 * pair : 128 * pair + 128] = jnp.concatenate(
            [rc_v[2 * pair], rc_v[2 * pair + 1]], axis=1
        )

    def expand(x, left, right, place):
        turned = jnp.concatenate([x[:, RANK:], x[:, :RANK]], axis=1)
        left[place] = x * left_mask
        right[place + 1] = x * right_mask
        left[place + 1] = turned * left_mask
        right[place] = turned * right_mask

    for pair in range(LEAVES // 2):
        expand(points_v[:, 128 * pair : 128 * pair + 128], near_left, near_right, BORDER + 2 * pair)
    window = 2 * LEAVES
    near_left[window] = jnp.zeros((RHS, 128), BF)
    near_right[window] = jnp.zeros((RHS, 128), BF)

    @pl.when(before < GY - 1)
    def _():
        pl.semaphore_wait(ready, GY - 1 - before)

    spread_gy(root_buf, 1)
    next_gy = (gx, (gy + 1) & (GY - 1))
    last_gy = (gx, (gy - 1) & (GY - 1))
    half = BORDER * RANK
    halos = []
    for place, (src, dst, device) in enumerate(
        (
            (points_v.at[:, pl.ds(half, half)], points_halo.at[0], next_gy),
            (points_v.at[:, pl.ds(0, half)], points_halo.at[1], last_gy),
        )
    ):
        halos.append(
            pltpu.make_async_remote_copy(
                src_ref=src,
                dst_ref=dst,
                send_sem=halo_send.at[place],
                recv_sem=halo_recv.at[place],
                device_id=device,
                device_id_type=MESH,
            )
        )
        halos[-1].start()

    @pl.when(gx < GX - 1)
    def _():
        answer_part(gx + 1, 0)
        send_coef(0, (gx + 1, gy)).start()

    lax.fori_loop(gx + 2, GX, answer_part, 0)
    lax.fori_loop(0, gx, wait_part, 0)
    lhs = [
        part_buf[2 * pair] * left_mask + part_buf[2 * pair + 1] * right_mask
        for pair in range(GX // 2)
    ]
    plane = dot_nt(jnp.concatenate(lhs, axis=1), pc_cat[...])
    high = plane.astype(BF).astype(F32)
    sum_buf[gy] = jnp.concatenate([high, plane - high], axis=1).astype(BF)
    spread_gy(sum_buf, 2)

    halos[0].wait_recv()
    halos[1].wait_recv()
    for side in range(2):
        for pair in range(BORDER // 2):
            expand(
                points_halo[side, :, 128 * pair : 128 * pair + 128],
                near_left,
                near_right,
                side * (BORDER + LEAVES) + 2 * pair,
            )
    load_near.wait()
    load_near_source.wait()
    load_near_count.wait()
    for c in range(CHUNKS):
        rows = []
        for leaf in range(4 * c, 4 * c + 4):
            count = near_count[leaf]
            places = []
            for slot in range(NEAR):
                place = near_source[slot, leaf] - first_leaf + BORDER
                place = jnp.minimum(jnp.maximum(place, 0), window - 1)
                places.append(jnp.where(slot < count, place, window))
            rows.append(
                jnp.concatenate(
                    [
                        near_left[places[0]] + near_right[places[1]],
                        near_left[places[2]] + near_right[places[3]],
                    ],
                    axis=1,
                )
            )
        full = dot_nt(jnp.concatenate(rows, axis=0), near_v[4 * c : 4 * c + 4].reshape(256, 256))
        near_rows[:, 256 * c : 256 * c + 256] = diagonal(full)

    @pl.when(gx > 0)
    def _():
        send_coef(0, (gx - 1, gy)).wait_recv()

    @pl.when(gx == 0)
    def _():
        coef_halo[0] = jnp.zeros((RHS, SPAN), BF)

    @pl.when(gx < GX - 1)
    def _():
        send_coef(1, (gx + 1, gy)).wait_recv()

    @pl.when(gx == GX - 1)
    def _():
        coef_halo[1] = jnp.zeros((RHS, SPAN), BF)

    for side in range(2):
        for pair in range(LEAVES // 2):
            expand(
                coef_halo[side, :, 128 * pair : 128 * pair + 128],
                far_left,
                far_right,
                side * LEAVES + 2 * pair,
            )
    load_far_source.wait()
    load_far_kind.wait()
    for c in range(CHUNKS):
        rows = []
        matrices = []
        for leaf in range(4 * c, 4 * c + 4):
            places = []
            kinds = []
            for slot in range(FAR):
                source = far_source[slot, leaf] - first_leaf
                place = jnp.where(
                    source < 0, source + GY * LEAVES, source - GY * LEAVES + LEAVES
                )
                places.append(jnp.minimum(jnp.maximum(place, 0), window - 1))
                kinds.append(far_kind[slot, leaf])
            rows.append(
                jnp.concatenate(
                    [
                        far_left[places[0]] + far_right[places[1]],
                        far_left[places[2]] + far_right[places[3]],
                    ],
                    axis=1,
                )
            )
            matrices.append(
                jnp.concatenate(
                    [
                        kind_left[kinds[0]] + kind_right[kinds[1]],
                        kind_left[kinds[2]] + kind_right[kinds[3]],
                    ],
                    axis=1,
                )
            )
        full = dot_nt(jnp.concatenate(rows, axis=0), jnp.concatenate(matrices, axis=0))
        far_rows[:, 256 * c : 256 * c + 256] = diagonal(full)

    wait_all(gather_recv.at[1], root_buf, GY - 1)
    load_root_source.wait()
    chosen = [
        root_buf[root_source[0, 2 * pair]] * left_mask
        + root_buf[root_source[0, 2 * pair + 1]] * right_mask
        for pair in range(ROOT_SLOTS // 2)
    ]
    beside = dot_nt(jnp.concatenate(chosen, axis=1), rc_cat[...])
    beside = jnp.where(root_keep, beside, 0.0).astype(BF)

    load_row.wait()
    load_down.wait()
    load_pd.wait()
    unit = (
        lax.broadcasted_iota(jnp.int32, (RANK, RANK), 0)
        == lax.broadcasted_iota(jnp.int32, (RANK, RANK), 1)
    )
    plane_turned = dot_nt(unit.astype(F32).astype(BF), pd_v[...])
    keep_root = lax.broadcasted_iota(jnp.int32, (RANK, RANK), 1) < root_rank[0]
    plane_turned = jnp.where(keep_root, plane_turned, 0.0).astype(BF)
    downward = jnp.concatenate([beside, plane_turned], axis=0)
    for c in range(CHUNKS):
        span = slice(256 * c, 256 * c + 256)
        leaf_out = dot_nt(downward, down_v[4 * c : 4 * c + 4].reshape(256, RANK))
        leaf_out = jnp.concatenate(
            [leaf_out[:RHS] + far_rows[:, span], leaf_out[RHS:]], axis=0
        )
        keep = jnp.concatenate([keep_lanes[:, span]] * 10, axis=0)
        leaf_out = jnp.where(keep > 0.0, leaf_out, 0.0).astype(BF)
        values = dot_nn(leaf_out, block_diag(row_v[:, span]))
        near_rows[:, span] += values[:RHS]
        plane_map[:, span] = values[RHS:].astype(BF)

    wait_all(gather_recv.at[2], sum_buf, GY - 1)
    total = [sum_buf[q].astype(F32) for q in range(GY)]
    while len(total) > 1:
        total = [a + b for a, b in zip(total[0::2], total[1::2])]
    plane_out = (total[0][:, :RANK] + total[0][:, RANK:]).astype(BF)
    for c in range(CHUNKS):
        span = slice(256 * c, 256 * c + 256)
        out[:, span] = (near_rows[:, span] + dot_nn(plane_out, plane_map[:, span])).astype(BF)

    for halo in halos:
        halo.wait_send()

    @pl.when(gx > 0)
    def _():
        send_coef(1, (gx - 1, gy)).wait_send()

    @pl.when(gx < GX - 1)
    def _():
        send_coef(0, (gx + 1, gy)).wait_send()

    wait_all(gather_send.at[0], part_buf, GX - 1)
    wait_all(gather_send.at[1], root_buf, GY - 1)
    wait_all(gather_send.at[2], sum_buf, GY - 1)


def per_device(
    points_in,
    near_blocks,
    near_source,
    near_count,
    col_basis,
    row_basis,
    up_transfer,
    down_transfer,
    leaf_rank,
    kind_table,
    far_source,
    far_kind,
    root_rank,
    root_coupling,
    root_source,
    plane_up,
    plane_down,
    plane_coupling,
):
    hbm = pl.BlockSpec(memory_space=pltpu.HBM)
    return pl.pallas_call(
        kernel,
        out_shape=jax.ShapeDtypeStruct((RHS, SPAN), BF),
        in_specs=[hbm] * 16 + [pl.BlockSpec(memory_space=pltpu.SMEM), hbm],
        out_specs=pl.BlockSpec(memory_space=pltpu.VMEM),
        scratch_shapes=[
            pltpu.SMEM((NEAR, LEAVES), jnp.int32),
            pltpu.SMEM((LEAVES,), jnp.int32),
            pltpu.SMEM((LEAVES,), jnp.int32),
            pltpu.SMEM((FAR, LEAVES), jnp.int32),
            pltpu.SMEM((FAR, LEAVES), jnp.int32),
            pltpu.SMEM((1, ROOT_SLOTS), jnp.int32),
            pltpu.VMEM((RHS, SPAN), BF),
            pltpu.VMEM((RANK, SPAN), BF),
            pltpu.VMEM((LEAVES, RANK, RANK), BF),
            pltpu.VMEM((RANK, RANK), BF),
            pltpu.VMEM((GX, RANK, RANK), BF),
            pltpu.VMEM((LEAVES, RANK, NEAR * RANK), BF),
            pltpu.VMEM((KINDS, RANK, RANK), BF),
            pltpu.VMEM((RANK, SPAN), BF),
            pltpu.VMEM((ROOT_SLOTS, RANK, RANK), BF),
            pltpu.VMEM((LEAVES, RANK, RANK), BF),
            pltpu.VMEM((RANK, RANK), BF),
            pltpu.VMEM((2, RHS, BORDER * RANK), BF),
            pltpu.VMEM((RHS, SPAN), BF),
            pltpu.VMEM((2, RHS, SPAN), BF),
            pltpu.VMEM((GX, RHS, 128), BF),
            pltpu.VMEM((GY, RHS, 128), BF),
            pltpu.VMEM((GY, RHS, 128), BF),
            pltpu.VMEM((2 * LEAVES + 1, RHS, 128), BF),
            pltpu.VMEM((2 * LEAVES + 1, RHS, 128), BF),
            pltpu.VMEM((2 * LEAVES, RHS, 128), BF),
            pltpu.VMEM((2 * LEAVES, RHS, 128), BF),
            pltpu.VMEM((KINDS, RANK, 128), BF),
            pltpu.VMEM((KINDS, RANK, 128), BF),
            pltpu.VMEM((RANK, GX * RANK), BF),
            pltpu.VMEM((RANK, ROOT_SLOTS * RANK), BF),
            pltpu.VMEM((RANK, SPAN), BF),
            pltpu.VMEM((8, SPAN), F32),
            pltpu.VMEM((RHS, SPAN), F32),
            pltpu.VMEM((RHS, SPAN), F32),
            pltpu.SemaphoreType.DMA((17,)),
            pltpu.SemaphoreType.DMA((4,)),
            pltpu.SemaphoreType.DMA((4,)),
            pltpu.SemaphoreType.DMA((3,)),
            pltpu.SemaphoreType.DMA((3,)),
            pltpu.SemaphoreType.DMA((GX,)),
            pltpu.SemaphoreType.REGULAR,
        ],
        compiler_params=pltpu.CompilerParams(
            collective_id=0, has_side_effects=True, vmem_limit_bytes=32 * 2**20
        ),
        name="h2_product",
    )(
        *(
            array if array.size == 1 else pltpu.with_memory_space_constraint(array, pltpu.HBM)
            for array in (
                points_in,
                col_basis,
                up_transfer,
                plane_up,
                plane_coupling,
                near_blocks,
                kind_table,
                row_basis,
                root_coupling,
                down_transfer,
                plane_down,
                near_source.T,
                near_count,
                leaf_rank,
                far_source.T,
                far_kind.T,
                root_rank,
                root_source,
            )
        )
    )


def solution(mesh):
    return jax.shard_map(
        per_device,
        mesh=mesh,
        in_specs=(
            P(None, ("gx", "gy")),
            P(("gx", "gy"), None, None),
            P(("gx", "gy"), None),
            P(("gx", "gy")),
            P(None, ("gx", "gy")),
            P(None, ("gx", "gy")),
            P(("gx", "gy"), None, None),
            P(("gx", "gy"), None, None),
            P(("gx", "gy")),
            P(),
            P(("gx", "gy"), None),
            P(("gx", "gy"), None),
            P(("gx", "gy")),
            P(("gx", "gy"), None, None, None),
            P(("gx", "gy"), None),
            P(("gx", "gy"), None, None),
            P(("gx", "gy"), None, None),
            P("gx", None, None, None),
        ),
        out_specs=P(None, ("gx", "gy")),
        check_vma=False,
    )
```

```python
import jax
import jax.numpy as jnp
from jax import lax
from jax.experimental import pallas as pl
from jax.experimental.pallas import tpu as pltpu
from jax.sharding import PartitionSpec as P

MESH = pl.DeviceIdType.MESH
BF = jnp.bfloat16
F32 = jnp.float32

RHS = 16
LEAVES = 32
RANK = 64
BORDER = 16
GX = 16
GY = 32
NEAR = 4
FAR = 4
KINDS = 16
ROOT_SLOTS = 8
CHUNKS = 8
SPAN = LEAVES * RANK


def dot_nt(a, b):
    return lax.dot_general(a, b, (((1,), (1,)), ((), ())), preferred_element_type=F32)


def dot_nn(a, b):
    return lax.dot_general(a, b, (((1,), (0,)), ((), ())), preferred_element_type=F32)


def place_of(gy):
    x, y = gy >> 3, gy & 7
    turned = (y if y < 4 else 11 - y) if isinstance(y, int) else jnp.where(y < 4, y, 11 - y)
    return ((turned + x) << 5) + gy


def kernel(
    points,
    col,
    up,
    plane_up,
    plane_coupling,
    near_blocks,
    kind_table,
    row,
    root_coupling,
    down,
    plane_down,
    near_source_h,
    near_count_h,
    leaf_rank_h,
    far_source_h,
    far_kind_h,
    root_rank,
    root_source_h,
    out,
    near_source,
    near_count,
    leaf_rank,
    far_source,
    far_kind,
    root_source,
    points_v,
    col_v,
    up_v,
    pu_v,
    pc_v,
    near_v,
    kind_v,
    row_v,
    rc_v,
    down_v,
    pd_v,
    points_halo,
    coef,
    coef_halo,
    part_buf,
    root_buf,
    sum_buf,
    near_left,
    near_right,
    far_left,
    far_right,
    kind_left,
    kind_right,
    pc_cat,
    rc_cat,
    plane_map,
    keep_lanes,
    far_rows,
    near_rows,
    load_sem,
    halo_send,
    halo_recv,
    gather_send,
    gather_recv,
    part_recv,
    ready,
):
    gx = lax.axis_index("gx")
    gy = lax.axis_index("gy")
    first_leaf = (gx * GY + gy) * LEAVES

    pairs = (
        (leaf_rank_h, leaf_rank),
        (points, points_v),
        (col, col_v),
        (up, up_v),
        (plane_up.at[0], pu_v),
        (plane_coupling.at[0], pc_v),
        (near_source_h, near_source),
        (near_count_h, near_count),
        (near_blocks, near_v),
        (kind_table, kind_v),
        (row, row_v),
        (root_coupling.at[0], rc_v),
        (down, down_v),
        (plane_down.at[0], pd_v),
        (far_source_h, far_source),
        (far_kind_h, far_kind),
        (root_source_h, root_source),
    )
    loads = [
        pltpu.make_async_copy(src, dst, load_sem.at[place])
        for place, (src, dst) in enumerate(pairs)
    ]
    (
        load_leaf_rank,
        load_points,
        load_col,
        load_up,
        load_pu,
        load_pc,
        load_near_source,
        load_near_count,
        load_near,
        load_kind,
        load_row,
        load_rc,
        load_down,
        load_pd,
        load_far_source,
        load_far_kind,
        load_root_source,
    ) = loads
    for load in loads[:5]:
        load.start()

    barrier = pltpu.get_barrier_semaphore()

    def greet_gx(i, carry):
        pl.semaphore_signal(
            barrier, inc=1, device_id=(i, gy), device_id_type=MESH
        )
        return carry

    my_place = place_of(gy)

    def greet_gy(i, before):
        @pl.when(place_of(i) > my_place)
        def _():
            pl.semaphore_signal(barrier, inc=1, device_id=(gx, i), device_id_type=MESH)

        return before + jnp.where(place_of(i) < my_place, 1, 0)

    def greet_gy_back(i, carry):
        @pl.when(place_of(i) < my_place)
        def _():
            pl.semaphore_signal(ready, inc=1, device_id=(gx, i), device_id_type=MESH)

        return carry

    lax.fori_loop(gx + 1, GX, greet_gx, 0)
    before = 0
    for peer in range(GY):
        before = greet_gy(peer, before)

    lane = lax.broadcasted_iota(jnp.int32, (RHS, 128), 1)
    low = lane < RANK
    left_mask = low.astype(F32).astype(BF)
    right_mask = (lane >= RANK).astype(F32).astype(BF)
    lane_leaf = lax.broadcasted_iota(jnp.int32, (RANK, 256), 1) // RANK
    leaf_masks = [(lane_leaf == i).astype(F32).astype(BF) for i in range(4)]

    def block_diag(block):
        return jnp.concatenate([block * mask for mask in leaf_masks], axis=0)

    def diagonal(full):
        first = jnp.where(low, full[0:16, 0:128], full[16:32, 0:128])
        second = jnp.where(low, full[32:48, 128:256], full[48:64, 128:256])
        return jnp.concatenate([first, second], axis=1)

    lane_rank = lax.broadcasted_iota(jnp.int32, (8, 128), 1)
    in_low = lane_rank < RANK
    rank_of_lane = jnp.where(in_low, lane_rank, lane_rank - RANK)
    load_leaf_rank.wait()
    for pair in range(LEAVES // 2):
        ranks = jnp.where(in_low, leaf_rank[2 * pair], leaf_rank[2 * pair + 1])
        keep_lanes[:, 128 * pair : 128 * pair + 128] = (rank_of_lane < ranks).astype(F32)

    load_points.wait()
    load_col.wait()
    for c in range(CHUNKS):
        span = slice(256 * c, 256 * c + 256)
        full = dot_nt(points_v[:, span], block_diag(col_v[:, span]))
        keep = jnp.concatenate([keep_lanes[:, span]] * 2, axis=0)
        coef[:, span] = jnp.where(keep > 0.0, full, 0.0).astype(BF)

    load_up.wait()
    load_pu.wait()
    for load in loads[5:]:
        load.start()
    root = jnp.zeros((RHS, RANK), F32)
    for c in range(CHUNKS):
        root = root + dot_nn(
            coef[:, 256 * c : 256 * c + 256], up_v[4 * c : 4 * c + 4].reshape(256, RANK)
        )
    root_keep = lax.broadcasted_iota(jnp.int32, (RHS, RANK), 1) < root_rank[0]
    root = jnp.where(root_keep, root, 0.0)
    part = dot_nn(root.astype(BF), pu_v[...])
    part_buf[gx] = jnp.concatenate([part, part], axis=1).astype(BF)
    root_buf[gy] = jnp.concatenate([root, root], axis=1).astype(BF)

    @pl.when(gx + before > 0)
    def _():
        pl.semaphore_wait(barrier, gx + before)

    def send_part(peer, carry):
        pltpu.make_async_remote_copy(
            src_ref=part_buf.at[gx],
            dst_ref=part_buf.at[gx],
            send_sem=gather_send.at[0],
            recv_sem=part_recv.at[gx],
            device_id=(peer, gy),
            device_id_type=MESH,
        ).start()
        return carry

    def wait_part(peer, carry):
        held = part_buf.at[peer]
        pltpu.make_async_copy(held, held, part_recv.at[peer]).wait()
        return carry

    def answer_part(peer, carry):
        wait_part(peer, carry)
        return send_part(peer, carry)

    def send_coef(side, device):
        return pltpu.make_async_remote_copy(
            src_ref=coef,
            dst_ref=coef_halo.at[side],
            send_sem=halo_send.at[2 + side],
            recv_sem=halo_recv.at[2 + side],
            device_id=device,
            device_id_type=MESH,
        )

    def spread_gy(buf, place):
        def send(i, carry):
            peer = i + ((i - gy + GY) >> 5)
            pltpu.make_async_remote_copy(
                src_ref=buf.at[gy],
                dst_ref=buf.at[gy],
                send_sem=gather_send.at[place],
                recv_sem=gather_recv.at[place],
                device_id=(gx, peer),
                device_id_type=MESH,
            ).start()
            return carry

        lax.fori_loop(0, GY - 1, send, 0)

    def wait_all(sem, buf, count):
        held = buf.at[pl.ds(0, count)]
        pltpu.make_async_copy(held, held, sem).wait()

    lax.fori_loop(0, gx, send_part, 0)
    for peer in range(GY):
        greet_gy_back(peer, 0)

    @pl.when(gx > 0)
    def _():
        send_coef(1, (gx - 1, gy)).start()


    load_pc.wait()
    for pair in range(GX // 2):
        blocks = []
        for q in (2 * pair, 2 * pair + 1):
            far = (jnp.abs(gx - q) >= 2).astype(F32).astype(BF)
            blocks.append(pc_v[q] * far)
        pc_cat[:, 128 * pair : 128 * pair + 128] = jnp.concatenate(blocks, axis=1)
    load_kind.wait()
    zero_block = jnp.zeros((RANK, RANK), BF)
    for t in range(KINDS):
        kind_left[t] = jnp.concatenate([kind_v[t], zero_block], axis=1)
        kind_right[t] = jnp.concatenate([zero_block, kind_v[t]], axis=1)
    load_rc.wait()
    for pair in range(ROOT_SLOTS // 2):
        rc_cat[:, 128 * pair : 128 * pair + 128] = jnp.concatenate(
            [rc_v[2 * pair], rc_v[2 * pair + 1]], axis=1
        )

    def expand(x, left, right, place):
        turned = jnp.concatenate([x[:, RANK:], x[:, :RANK]], axis=1)
        left[place] = x * left_mask
        right[place + 1] = x * right_mask
        left[place + 1] = turned * left_mask
        right[place] = turned * right_mask

    for pair in range(LEAVES // 2):
        expand(points_v[:, 128 * pair : 128 * pair + 128], near_left, near_right, BORDER + 2 * pair)
    window = 2 * LEAVES
    near_left[window] = jnp.zeros((RHS, 128), BF)
    near_right[window] = jnp.zeros((RHS, 128), BF)

    @pl.when(before < GY - 1)
    def _():
        pl.semaphore_wait(ready, GY - 1 - before)

    spread_gy(root_buf, 1)
    next_gy = (gx, (gy + 1) & (GY - 1))
    last_gy = (gx, (gy - 1) & (GY - 1))
    half = BORDER * RANK
    halos = []
    for place, (src, dst, device) in enumerate(
        (
            (points_v.at[:, pl.ds(half, half)], points_halo.at[0], next_gy),
            (points_v.at[:, pl.ds(0, half)], points_halo.at[1], last_gy),
        )
    ):
        halos.append(
            pltpu.make_async_remote_copy(
                src_ref=src,
                dst_ref=dst,
                send_sem=halo_send.at[place],
                recv_sem=halo_recv.at[place],
                device_id=device,
                device_id_type=MESH,
            )
        )
        halos[-1].start()

    @pl.when(gx < GX - 1)
    def _():
        answer_part(gx + 1, 0)
        send_coef(0, (gx + 1, gy)).start()

    lax.fori_loop(gx + 2, GX, answer_part, 0)
    lax.fori_loop(0, gx, wait_part, 0)
    lhs = [
        part_buf[2 * pair] * left_mask + part_buf[2 * pair + 1] * right_mask
        for pair in range(GX // 2)
    ]
    plane = dot_nt(jnp.concatenate(lhs, axis=1), pc_cat[...])
    high = plane.astype(BF).astype(F32)
    sum_buf[gy] = jnp.concatenate([high, plane - high], axis=1).astype(BF)
    spread_gy(sum_buf, 2)

    halos[0].wait_recv()
    halos[1].wait_recv()
    for side in range(2):
        for pair in range(BORDER // 2):
            expand(
                points_halo[side, :, 128 * pair : 128 * pair + 128],
                near_left,
                near_right,
                side * (BORDER + LEAVES) + 2 * pair,
            )
    load_near.wait()
    load_near_source.wait()
    load_near_count.wait()
    for c in range(CHUNKS):
        rows = []
        for leaf in range(4 * c, 4 * c + 4):
            count = near_count[leaf]
            places = []
            for slot in range(NEAR):
                place = near_source[slot, leaf] - first_leaf + BORDER
                place = jnp.minimum(jnp.maximum(place, 0), window - 1)
                places.append(jnp.where(slot < count, place, window))
            rows.append(
                jnp.concatenate(
                    [
                        near_left[places[0]] + near_right[places[1]],
                        near_left[places[2]] + near_right[places[3]],
                    ],
                    axis=1,
                )
            )
        full = dot_nt(jnp.concatenate(rows, axis=0), near_v[4 * c : 4 * c + 4].reshape(256, 256))
        near_rows[:, 256 * c : 256 * c + 256] = diagonal(full)

    @pl.when(gx > 0)
    def _():
        send_coef(0, (gx - 1, gy)).wait_recv()

    @pl.when(gx == 0)
    def _():
        coef_halo[0] = jnp.zeros((RHS, SPAN), BF)

    @pl.when(gx < GX - 1)
    def _():
        send_coef(1, (gx + 1, gy)).wait_recv()

    @pl.when(gx == GX - 1)
    def _():
        coef_halo[1] = jnp.zeros((RHS, SPAN), BF)

    for side in range(2):
        for pair in range(LEAVES // 2):
            expand(
                coef_halo[side, :, 128 * pair : 128 * pair + 128],
                far_left,
                far_right,
                side * LEAVES + 2 * pair,
            )
    load_far_source.wait()
    load_far_kind.wait()
    for c in range(CHUNKS):
        rows = []
        matrices = []
        for leaf in range(4 * c, 4 * c + 4):
            places = []
            kinds = []
            for slot in range(FAR):
                source = far_source[slot, leaf] - first_leaf
                place = jnp.where(
                    source < 0, source + GY * LEAVES, source - GY * LEAVES + LEAVES
                )
                places.append(jnp.minimum(jnp.maximum(place, 0), window - 1))
                kinds.append(far_kind[slot, leaf])
            rows.append(
                jnp.concatenate(
                    [
                        far_left[places[0]] + far_right[places[1]],
                        far_left[places[2]] + far_right[places[3]],
                    ],
                    axis=1,
                )
            )
            matrices.append(
                jnp.concatenate(
                    [
                        kind_left[kinds[0]] + kind_right[kinds[1]],
                        kind_left[kinds[2]] + kind_right[kinds[3]],
                    ],
                    axis=1,
                )
            )
        full = dot_nt(jnp.concatenate(rows, axis=0), jnp.concatenate(matrices, axis=0))
        far_rows[:, 256 * c : 256 * c + 256] = diagonal(full)

    wait_all(gather_recv.at[1], root_buf, GY - 1)
    load_root_source.wait()
    chosen = [
        root_buf[root_source[0, 2 * pair]] * left_mask
        + root_buf[root_source[0, 2 * pair + 1]] * right_mask
        for pair in range(ROOT_SLOTS // 2)
    ]
    beside = dot_nt(jnp.concatenate(chosen, axis=1), rc_cat[...])
    beside = jnp.where(root_keep, beside, 0.0).astype(BF)

    load_row.wait()
    load_down.wait()
    load_pd.wait()
    unit = (
        lax.broadcasted_iota(jnp.int32, (RANK, RANK), 0)
        == lax.broadcasted_iota(jnp.int32, (RANK, RANK), 1)
    )
    plane_turned = dot_nt(unit.astype(F32).astype(BF), pd_v[...])
    keep_root = lax.broadcasted_iota(jnp.int32, (RANK, RANK), 1) < root_rank[0]
    plane_turned = jnp.where(keep_root, plane_turned, 0.0).astype(BF)
    downward = jnp.concatenate([beside, plane_turned], axis=0)
    for c in range(CHUNKS):
        span = slice(256 * c, 256 * c + 256)
        leaf_out = dot_nt(downward, down_v[4 * c : 4 * c + 4].reshape(256, RANK))
        leaf_out = jnp.concatenate(
            [leaf_out[:RHS] + far_rows[:, span], leaf_out[RHS:]], axis=0
        )
        keep = jnp.concatenate([keep_lanes[:, span]] * 10, axis=0)
        leaf_out = jnp.where(keep > 0.0, leaf_out, 0.0).astype(BF)
        values = dot_nn(leaf_out, block_diag(row_v[:, span]))
        near_rows[:, span] += values[:RHS]
        plane_map[:, span] = values[RHS:].astype(BF)

    wait_all(gather_recv.at[2], sum_buf, GY - 1)
    total = [sum_buf[q].astype(F32) for q in range(GY)]
    while len(total) > 1:
        total = [a + b for a, b in zip(total[0::2], total[1::2])]
    plane_out = (total[0][:, :RANK] + total[0][:, RANK:]).astype(BF)
    for c in range(CHUNKS):
        span = slice(256 * c, 256 * c + 256)
        out[:, span] = (near_rows[:, span] + dot_nn(plane_out, plane_map[:, span])).astype(BF)

    for halo in halos:
        halo.wait_send()

    @pl.when(gx > 0)
    def _():
        send_coef(1, (gx - 1, gy)).wait_send()

    @pl.when(gx < GX - 1)
    def _():
        send_coef(0, (gx + 1, gy)).wait_send()

    wait_all(gather_send.at[0], part_buf, GX - 1)
    wait_all(gather_send.at[1], root_buf, GY - 1)
    wait_all(gather_send.at[2], sum_buf, GY - 1)


def per_device(
    points_in,
    near_blocks,
    near_source,
    near_count,
    col_basis,
    row_basis,
    up_transfer,
    down_transfer,
    leaf_rank,
    kind_table,
    far_source,
    far_kind,
    root_rank,
    root_coupling,
    root_source,
    plane_up,
    plane_down,
    plane_coupling,
):
    hbm = pl.BlockSpec(memory_space=pltpu.HBM)
    return pl.pallas_call(
        kernel,
        out_shape=jax.ShapeDtypeStruct((RHS, SPAN), BF),
        in_specs=[hbm] * 16 + [pl.BlockSpec(memory_space=pltpu.SMEM), hbm],
        out_specs=pl.BlockSpec(memory_space=pltpu.VMEM),
        scratch_shapes=[
            pltpu.SMEM((NEAR, LEAVES), jnp.int32),
            pltpu.SMEM((LEAVES,), jnp.int32),
            pltpu.SMEM((LEAVES,), jnp.int32),
            pltpu.SMEM((FAR, LEAVES), jnp.int32),
            pltpu.SMEM((FAR, LEAVES), jnp.int32),
            pltpu.SMEM((1, ROOT_SLOTS), jnp.int32),
            pltpu.VMEM((RHS, SPAN), BF),
            pltpu.VMEM((RANK, SPAN), BF),
            pltpu.VMEM((LEAVES, RANK, RANK), BF),
            pltpu.VMEM((RANK, RANK), BF),
            pltpu.VMEM((GX, RANK, RANK), BF),
            pltpu.VMEM((LEAVES, RANK, NEAR * RANK), BF),
            pltpu.VMEM((KINDS, RANK, RANK), BF),
            pltpu.VMEM((RANK, SPAN), BF),
            pltpu.VMEM((ROOT_SLOTS, RANK, RANK), BF),
            pltpu.VMEM((LEAVES, RANK, RANK), BF),
            pltpu.VMEM((RANK, RANK), BF),
            pltpu.VMEM((2, RHS, BORDER * RANK), BF),
            pltpu.VMEM((RHS, SPAN), BF),
            pltpu.VMEM((2, RHS, SPAN), BF),
            pltpu.VMEM((GX, RHS, 128), BF),
            pltpu.VMEM((GY, RHS, 128), BF),
            pltpu.VMEM((GY, RHS, 128), BF),
            pltpu.VMEM((2 * LEAVES + 1, RHS, 128), BF),
            pltpu.VMEM((2 * LEAVES + 1, RHS, 128), BF),
            pltpu.VMEM((2 * LEAVES, RHS, 128), BF),
            pltpu.VMEM((2 * LEAVES, RHS, 128), BF),
            pltpu.VMEM((KINDS, RANK, 128), BF),
            pltpu.VMEM((KINDS, RANK, 128), BF),
            pltpu.VMEM((RANK, GX * RANK), BF),
            pltpu.VMEM((RANK, ROOT_SLOTS * RANK), BF),
            pltpu.VMEM((RANK, SPAN), BF),
            pltpu.VMEM((8, SPAN), F32),
            pltpu.VMEM((RHS, SPAN), F32),
            pltpu.VMEM((RHS, SPAN), F32),
            pltpu.SemaphoreType.DMA((17,)),
            pltpu.SemaphoreType.DMA((4,)),
            pltpu.SemaphoreType.DMA((4,)),
            pltpu.SemaphoreType.DMA((3,)),
            pltpu.SemaphoreType.DMA((3,)),
            pltpu.SemaphoreType.DMA((GX,)),
            pltpu.SemaphoreType.REGULAR,
        ],
        compiler_params=pltpu.CompilerParams(
            collective_id=0, has_side_effects=True, vmem_limit_bytes=32 * 2**20
        ),
        name="h2_product",
    )(
        *(
            array if array.size == 1 else pltpu.with_memory_space_constraint(array, pltpu.HBM)
            for array in (
                points_in,
                col_basis,
                up_transfer,
                plane_up,
                plane_coupling,
                near_blocks,
                kind_table,
                row_basis,
                root_coupling,
                down_transfer,
                plane_down,
                near_source.T,
                near_count,
                leaf_rank,
                far_source.T,
                far_kind.T,
                root_rank,
                root_source,
            )
        )
    )


def solution(mesh):
    return jax.shard_map(
        per_device,
        mesh=mesh,
        in_specs=(
            P(None, ("gx", "gy")),
            P(("gx", "gy"), None, None),
            P(("gx", "gy"), None),
            P(("gx", "gy")),
            P(None, ("gx", "gy")),
            P(None, ("gx", "gy")),
            P(("gx", "gy"), None, None),
            P(("gx", "gy"), None, None),
            P(("gx", "gy")),
            P(),
            P(("gx", "gy"), None),
            P(("gx", "gy"), None),
            P(("gx", "gy")),
            P(("gx", "gy"), None, None, None),
            P(("gx", "gy"), None),
            P(("gx", "gy"), None, None),
            P(("gx", "gy"), None, None),
            P("gx", None, None, None),
        ),
        out_specs=P(None, ("gx", "gy")),
        check_vma=False,
    )
```
